32 devices in a mesh: tm: 4 (over x, core), tp: 8 (over z, y).
Axes of the slice: x: 2, y: 2, z: 4, core: 2. Of those that a mesh axis runs over, the one named last changes fastest.
Arguments:
- states: float32 [1024, 6144], P(('tm', 'tp')), may hold values from -6 to 6
- norm_gain: float32 [6144], replicated, may hold values from 0.5 to 1.5
- qkv_weight: bfloat16 [6144, 3, 4096], P(None, None, 'tp'), may hold values from -1 to 1
- qk_gain: float32 [2, 4096], P(None, 'tp'), may hold values from 1.2 to 5.5
- out_weight: bfloat16 [4096, 6144], P('tp'), may hold values from -0.09375 to 0.09375
- segment_lengths: int32 [4], replicated, may hold values from 1 to 256, 768 in all
Outputs:
- denoised: float32 [1024, 6144], P(('tm', 'tp'))
The draws below stay inside these ranges and needn't reach their ends.
Inputs may be any that keep to these rules, and one draw needn't show every extreme that they name: `segment_lengths`: the lengths sum to 768 and one segment is full.
All inputs are finite; a program needn't handle non-finite values.
Results may differ from the reference program's by a relative error of at most 0.015.
Values may be sent and summed in bfloat16 or wider, within the bound.
A program may use at most 128 MiB of HBM per device.

```python
import math
import jax
import jax.numpy as jnp
import numpy as np
from jax import lax

D = 6144
HEADS = 32
HD = 128
SEG = 256
STEPS = 2
TOKENS = 1024
N_TM = 4
N_TP = 8


def draw_qkv_weight(key, part):
    limit = math.sqrt(3.0 / D)
    first = jax.random.uniform(jax.random.fold_in(key, 11), (D, HEADS * HD), jnp.float32, -limit, limit)
    second = jax.random.uniform(jax.random.fold_in(key, 12), (D, HEADS * HD), jnp.float32, -limit, limit)
    third = jax.random.uniform(jax.random.fold_in(key, 13), (D, HEADS * HD), jnp.float32, -limit, limit)
    stacked = jnp.stack([first, second, third], axis=1)
    return stacked.astype(jnp.bfloat16)


def draw_qk_gain(key, part):
    gains = jnp.exp(jax.random.uniform(jax.random.fold_in(key, 23), (2, HEADS * HD), jnp.float32, math.log(1.2), math.log(2.2)))
    return gains


def steps_of(rng, shape, split, smallest, top_value):
    loudness, own = 1.0, jax.random.fold_in(rng, 6)
    for axis_at, blocks in split:
        heights = jnp.exp(jax.random.uniform(jax.random.fold_in(own, axis_at), (blocks,), jnp.float32, smallest / len(split), top_value / len(split)))
        loudness = loudness * jnp.repeat(heights, shape[axis_at] // blocks).reshape([-1 if axis == axis_at else 1 for axis in range(len(shape))])
    return loudness


def profile(number_of, total, most, slope):
    loads = [(1 << 20) // math.isqrt(standing ** slope) + 1 for standing in range(2, number_of + 1)]
    rest, given = total - most - (number_of - 1), [1] * (number_of - 1)
    while rest > 0:
        free = [i for i in range(number_of - 1) if given[i] < most]
        pool, left = sum([loads[i] for i in free]), rest
        for i in free:
            extra = min(most - given[i], max(1, left * loads[i] // pool), rest)
            given[i] = given[i] + extra
            rest = rest - extra
    return np.array([most] + given)


def uneven(key, count, total, reach, skew):
    if count == 2:
        one = jax.random.randint(key, (), max(1, total - reach), min(reach, total - 1) + 1)
        return jnp.stack([one, total - one])
    tallies = jnp.asarray(profile(count, total, reach, skew), jnp.int32)
    pairs = (count - 1) // 2
    giver, sink = tallies[1:1 + 2 * pairs:2], tallies[2:2 + 2 * pairs:2]
    slack = jnp.minimum(giver - 1, reach - sink)
    passed = jax.random.randint(jax.random.fold_in(key, 1), (pairs,), 0, 1 << 20) % (slack + 1)
    tallies = tallies.at[1:1 + 2 * pairs:2].set(giver - passed).at[2:2 + 2 * pairs:2].set(sink + passed)
    return tallies[jax.random.permutation(jax.random.fold_in(key, 2), count)]


def centred(stream_key, extent, scale, bound, pieces=(), held_as=jnp.bfloat16):
    loudness = steps_of(stream_key, extent, pieces, -0.22, 0.18) if pieces else 1.0
    result = jax.random.normal(stream_key, extent, jnp.float32) * scale * loudness
    return jnp.minimum(jnp.maximum(result, -bound), bound).astype(held_as)


def setup_inputs(seed: int = 0) -> dict:
    seeds = jax.random.split(jax.random.key(seed), 7)
    return {
        "states": centred(seeds[0], (TOKENS, D), 1.0, 6.0, ((0, 32),), jnp.float32),
        "norm_gain": jnp.clip(1.0 + 0.1 * jax.random.normal(seeds[1], (D,), jnp.float32), 0.5, 1.5),
        "qkv_weight": draw_qkv_weight(jax.random.fold_in(seeds[6], 71), 0),
        "qk_gain": draw_qk_gain(jax.random.fold_in(seeds[6], 71), 0),
        "out_weight": centred(seeds[4], (HEADS * HD, D), (HEADS * HD) ** -0.5, 0.09375, ((0, 8),)),
        "segment_lengths": uneven(seeds[5], N_TM, 3 * N_TM * SEG // 4, SEG, 1).astype(jnp.int32),
    }


eps_norm = 1e-06
step_size = -0.5

def rms_scale(values, gain):
    mean_square = lax.optimization_barrier(jnp.mean(values * values, axis=-1, keepdims=True))
    return values * lax.rsqrt(mean_square + eps_norm) * gain

def reference(states, norm_gain, qkv_weight, qk_gain, out_weight, segment_lengths):
    inner = HEADS * HD
    group_cols = inner // N_TP
    wmat = qkv_weight.reshape(D, 3 * inner)
    q_gain = qk_gain[0].reshape(HEADS, HD)
    k_gain = qk_gain[1].reshape(HEADS, HD)
    out_groups = out_weight.reshape(N_TP, group_cols, D).astype(jnp.float32)
    key_index = jnp.arange(TOKENS, dtype=jnp.int32)
    key_seg = key_index // SEG
    key_pos = key_index - key_seg * SEG
    key_len = segment_lengths[key_seg]
    current = states
    for step_index in range(STEPS):
        normed = rms_scale(current, norm_gain).astype(jnp.bfloat16)
        qkv = jnp.dot(normed, wmat, preferred_element_type=jnp.float32)
        queries = rms_scale(qkv[:, :inner].reshape(TOKENS, HEADS, HD), q_gain).astype(jnp.bfloat16)
        keys = rms_scale(qkv[:, inner:2 * inner].reshape(TOKENS, HEADS, HD), k_gain).astype(jnp.bfloat16)
        values = qkv[:, 2 * inner:].reshape(TOKENS, HEADS, HD).astype(jnp.bfloat16)
        keys_wide = keys.astype(jnp.float32)
        values_wide = values.astype(jnp.float32)

        def one_segment(seg_index):
            query_rows = lax.dynamic_slice_in_dim(queries, (seg_index * SEG).astype(jnp.int32), SEG, 0).astype(jnp.float32)
            scores = jnp.einsum('qhd,khd->hqk', query_rows, keys_wide) * HD ** (-0.5)
            valid = (key_seg <= seg_index) & (key_pos < key_len)
            masked = jnp.where(valid[None, None, :], scores, -1e+30)
            row_max = lax.optimization_barrier(jnp.max(masked, axis=-1, keepdims=True))
            expo = jnp.where(valid[None, None, :], jnp.exp(masked - row_max), 0.0)
            denom = lax.optimization_barrier(jnp.sum(expo, axis=-1))
            weights = expo.astype(jnp.bfloat16).astype(jnp.float32)
            summed = jnp.einsum('hqk,khd->qhd', weights, values_wide)
            attended = (summed / jnp.transpose(denom)[:, :, None]).astype(jnp.bfloat16)
            grouped = attended.reshape(SEG, N_TP, group_cols).astype(jnp.float32)
            partial_terms = jnp.einsum('sgk,gkd->gsd', grouped, out_groups)
            partial_terms = partial_terms.astype(jnp.bfloat16).astype(jnp.float32)
            return lax.optimization_barrier(jnp.sum(partial_terms, axis=0))
        velocity = lax.map(one_segment, jnp.arange(N_TM, dtype=jnp.int32)).reshape(TOKENS, D)
        current = current + step_size * velocity
    return current
```

```python
import functools

import jax
import jax.numpy as jnp
from jax import lax
from jax.experimental import pallas as pl
from jax.experimental.pallas import tpu as pltpu
from jax.sharding import PartitionSpec as P

HD = 128
STEPS = 2
GATHER_CHUNKS = 6
SCATTER_CHUNKS = 12

eps_norm = 1e-06
step_size = -0.5
BF16 = jnp.bfloat16
F32 = jnp.float32


def remote(src, dst, send_sem, recv_sem, tm, tp):
    return pltpu.make_async_remote_copy(
        src_ref=src,
        dst_ref=dst,
        send_sem=send_sem,
        recv_sem=recv_sem,
        device_id={"tm": tm, "tp": tp},
        device_id_type=pl.DeviceIdType.MESH,
    )


def loop(count, body):
    def step(index, carry):
        body(index)
        return carry

    lax.fori_loop(0, count, step, 0)


def kernel(
    tm_count, tp_count,
    states, gain, w_hbm, qk_gain, wo_hbm, bias,
    out,
    w, wo, hb, acc, qb, kv, att, run_max, run_sum, run_acc, pb, yb, ub, db,
    w_sem, wo_sem,
    h_recv, h_part, h_up, h_down,
    kv_recv, kv_sib, kv_chip, kv_fwd,
    y_send, y_recv, u_send, u_recv, d_send, d_recv,
):
    t, p = lax.axis_index("tm"), lax.axis_index("tp")
    lines, chips = tp_count // 2, tm_count // 2
    o, i = p // 2, p % 2
    ch, core = t // 2, t % 2
    partner, above, below = o * 2 + 1 - i, p + 2, p - 2
    sibling = ch * 2 + 1 - core
    has_above, has_below = o < lines - 1, o > 0
    rows, width = states.shape
    seg = rows * tp_count
    head_cols = w.shape[2]
    heads = head_cols // HD
    gw = width // GATHER_CHUNKS
    sw = width // SCATTER_CHUNKS

    def weight_copy(c):
        part = pl.ds(pl.multiple_of(c * gw, gw), gw)
        return pltpu.make_async_copy(w_hbm.at[:, part], w.at[:, part], w_sem.at[c])

    wo_copy = pltpu.make_async_copy(wo_hbm, wo, wo_sem)
    loop(GATHER_CHUNKS, lambda c: weight_copy(c).start())
    wo_copy.start()

    barrier = pltpu.get_barrier_semaphore()

    def greet(tm, tp):
        pl.semaphore_signal(
            barrier, inc=1, device_id={"tm": tm, "tp": tp}, device_id_type=pl.DeviceIdType.MESH
        )

    greet(t, partner)
    greet(sibling, p)

    @pl.when(has_above)
    def _():
        greet(t, above)

    @pl.when(has_below)
    def _():
        greet(t, below)

    for other in range(chips):

        @pl.when(other != ch)
        def _():
            greet(other * 2 + core, p)

    pl.semaphore_wait(
        barrier, 1 + chips + jnp.where(has_above, 1, 0) + jnp.where(has_below, 1, 0)
    )

    out[...] = states[...]

    def h_copy(c, line, side, send_sem, tp):
        ref = hb.at[c, line, side]
        return remote(ref, ref, send_sem.at[c, line], h_recv.at[c, line, side], t, tp)

    def h_wait(c, line, side):
        h_copy(c, line, side, h_part, partner).wait_recv()

    def kv_copy(s, seg_at, h, send_sem, tm):
        ref = kv.at[s, seg_at, h]
        return remote(ref, ref, send_sem, kv_recv.at[s, seg_at, h], tm, p)

    def flash(s, h, g, first):
        scores = lax.dot_general(
            qb[h], kv[s, g, h, 0], (((1,), (1,)), ((), ())), preferred_element_type=F32
        ) * HD ** (-0.5) + bias[g]
        top = jnp.max(scores, axis=-1, keepdims=True)
        if not first:
            old_top = run_max[h][:, :1]
            top = jnp.maximum(old_top, top)
        expo = jnp.exp(scores - top)
        total = jnp.sum(expo, axis=-1, keepdims=True)
        update = jnp.dot(expo.astype(BF16), kv[s, g, h, 1], preferred_element_type=F32)
        if not first:
            fade = jnp.exp(old_top - top)
            total = total + run_sum[h][:, :1] * fade
            update = update + run_acc[h] * fade
        run_max[h] = jnp.broadcast_to(top, (seg, HD))
        run_sum[h] = jnp.broadcast_to(total, (seg, HD))
        run_acc[h] = update

    def y_copy(c):
        return remote(
            pb.at[c, :, 1 - i], yb.at[c], y_send.at[c], y_recv.at[c], t, partner
        )

    def u_copy(c, line):
        return remote(
            pb.at[c, line, i], ub.at[c, line], u_send.at[c, line], u_recv.at[c, line], t, above
        )

    def d_copy(c, line):
        return remote(
            pb.at[c, line, i], db.at[c, line], d_send.at[c, line], d_recv.at[c, line], t, below
        )

    def step(s):
        square = jnp.zeros((rows, 1), F32)
        for c in range(GATHER_CHUNKS):
            x = out[:, c * gw : (c + 1) * gw]
            square = square + jnp.sum(x * x, axis=-1, keepdims=True)
        scale = lax.rsqrt(square / width + eps_norm)
        for c in range(GATHER_CHUNKS):
            part = slice(c * gw, (c + 1) * gw)
            hb[c, o, i] = (out[:, part] * scale * gain[:, part]).astype(BF16)

            @pl.when(has_above)
            def _():
                h_copy(c, o, i, h_up, above).start()

            @pl.when(has_below)
            def _():
                h_copy(c, o, i, h_down, below).start()

            h_copy(c, o, i, h_part, partner).start()

        for distance in range(1, lines):

            def forward(c):
                @pl.when(o >= distance)
                def _():
                    line = o - distance
                    h_wait(c, line, i)

                    @pl.when(has_above)
                    def _():
                        h_copy(c, line, i, h_up, above).start()

                    h_copy(c, line, i, h_part, partner).start()

                @pl.when(o + distance < lines)
                def _():
                    line = o + distance
                    h_wait(c, line, i)

                    @pl.when(has_below)
                    def _():
                        h_copy(c, line, i, h_down, below).start()

                    h_copy(c, line, i, h_part, partner).start()

            loop(GATHER_CHUNKS, forward)

        acc[...] = jnp.zeros_like(acc)

        def project(c):
            for line in range(lines):
                h_wait(c, line, 1 - i)

            @pl.when(s == 0)
            def _():
                weight_copy(c).wait()

            part = pl.ds(pl.multiple_of(c * gw, gw), gw)
            h = hb[c].reshape(seg, gw)
            for j in range(3):
                acc[j] += jnp.dot(h, w[j, part, :], preferred_element_type=F32)

        loop(GATHER_CHUNKS, project)

        for h in range(heads):
            cols = slice(h * HD, (h + 1) * HD)
            k = acc[1, :, cols]
            k_scale = lax.rsqrt(jnp.mean(k * k, axis=-1, keepdims=True) + eps_norm)
            kv[s, t, h, 0] = (k * k_scale * qk_gain[1:2, cols]).astype(BF16)
            kv[s, t, h, 1] = acc[2, :, cols].astype(BF16)
            for other in range(chips):

                @pl.when(other > ch)
                def _():
                    kv_copy(s, t, h, kv_chip.at[h, other], other * 2 + core).start()

            @pl.when(core == 0)
            def _():
                kv_copy(s, t, h, kv_sib.at[h], sibling).start()

        for h in range(heads):
            cols = slice(h * HD, (h + 1) * HD)
            q = acc[0, :, cols]
            q_scale = lax.rsqrt(jnp.mean(q * q, axis=-1, keepdims=True) + eps_norm)
            qb[h] = (q * q_scale * qk_gain[0:1, cols]).astype(BF16)
            flash(s, h, t, True)

        @pl.when(s == 0)
        def _():
            wo_copy.wait()

        def gather_sends(c):
            def one(line):
                h_copy(c, line, i, h_part, partner).wait_send()

                @pl.when(jnp.logical_and(has_above, line <= o))
                def _():
                    h_copy(c, line, i, h_up, above).wait_send()

                @pl.when(jnp.logical_and(has_below, line >= o))
                def _():
                    h_copy(c, line, i, h_down, below).wait_send()

            loop(lines, one)

        loop(GATHER_CHUNKS, gather_sends)

        for h in range(heads):
            cols = slice(h * HD, (h + 1) * HD)

            @pl.when(core == 1)
            def _():
                kv_copy(s, t - 1, h, kv_sib.at[h], sibling).wait_recv()
                flash(s, h, t - 1, False)

            def direct(other):
                @pl.when(other < ch)
                def _():
                    g = other * 2 + core
                    got = kv_copy(s, g, h, kv_fwd.at[h, other], sibling)
                    got.wait_recv()
                    got.start()
                    flash(s, h, g, False)

            def passed(other):
                @pl.when(other < ch)
                def _():
                    g = other * 2 + 1 - core
                    kv_copy(s, g, h, kv_fwd.at[h, other], sibling).wait_recv()
                    flash(s, h, g, False)

            loop(chips, direct)
            loop(chips, passed)
            att[:, cols] = (run_acc[h] / run_sum[h]).astype(BF16)

        def partial(c):
            part = pl.ds(pl.multiple_of(c * sw, sw), sw)
            product = jnp.dot(att[...], wo[:, part], preferred_element_type=F32)
            pb[c] = product.astype(BF16).reshape(lines, 2, rows, sw)
            y_copy(c).start()

        loop(SCATTER_CHUNKS, partial)

        def send_up(c):
            for line in range(1, lines):

                @pl.when(line > o)
                def _():
                    u_copy(c, line).start()

        def send_down(c):
            for line in range(lines - 1):

                @pl.when(line < o)
                def _():
                    d_copy(c, line).start()

        def paired(c):
            y_copy(c).wait_recv()
            pb[c, :, i] = (pb[c, :, i].astype(F32) + yb[c].astype(F32)).astype(BF16)

            @pl.when(o == 0)
            def _():
                send_up(c)

            @pl.when(o == lines - 1)
            def _():
                send_down(c)

        def hop(c):
            for line in range(1, lines):

                @pl.when(line > o)
                def _():
                    u_copy(c, line).wait_recv()
                    pb[c, line, i] = (
                        pb[c, line, i].astype(F32) + ub[c, line].astype(F32)
                    ).astype(BF16)
                    u_copy(c, line).start()

        def hop_down(c):
            for line in range(lines - 1):

                @pl.when(line < o)
                def _():
                    d_copy(c, line).wait_recv()
                    pb[c, line, i] = (
                        pb[c, line, i].astype(F32) + db[c, line].astype(F32)
                    ).astype(BF16)
                    d_copy(c, line).start()

        def finish(c):
            part = pl.ds(pl.multiple_of(c * sw, sw), sw)
            out[:, part] += step_size * pb[c, o, i].astype(F32)

            @pl.when(has_below)
            def _():
                u_copy(c, o).wait_recv()
                out[:, part] += step_size * ub[c, o].astype(F32)

            @pl.when(has_above)
            def _():
                d_copy(c, o).wait_recv()
                out[:, part] += step_size * db[c, o].astype(F32)

        def tick(at):
            @pl.when(at < SCATTER_CHUNKS)
            def _():
                paired(at)

            for k in range(1, lines):
                c = at - k
                live = jnp.logical_and(c >= 0, c < SCATTER_CHUNKS)
                if k < lines - 1:

                    @pl.when(jnp.logical_and(live, o == k))
                    def _():
                        hop(c)

                    @pl.when(jnp.logical_and(live, lines - 1 - o == k))
                    def _():
                        hop_down(c)
                else:

                    @pl.when(live)
                    def _():
                        finish(c)

        loop(SCATTER_CHUNKS + lines - 1, tick)

        def scatter_sends(c):
            y_copy(c).wait_send()

            def one(line):
                @pl.when(jnp.logical_and(has_above, line > o))
                def _():
                    u_copy(c, line).wait_send()

                @pl.when(jnp.logical_and(has_below, line < o))
                def _():
                    d_copy(c, line).wait_send()

            loop(lines, one)

        loop(SCATTER_CHUNKS, scatter_sends)
        for h in range(heads):

            @pl.when(core == 0)
            def _():
                kv_copy(s, t, h, kv_sib.at[h], sibling).wait_send()

            def chip_sends(other):
                @pl.when(other > ch)
                def _():
                    kv_copy(s, t, h, kv_chip.at[h, other], other * 2 + core).wait_send()

                @pl.when(other < ch)
                def _():
                    kv_copy(s, other * 2 + core, h, kv_fwd.at[h, other], sibling).wait_send()

            loop(chips, chip_sends)

    loop(STEPS, step)


def shards(states, norm_gain, qkv_weight, qk_gain, out_weight, segment_lengths):
    tm_count, tp_count = lax.axis_size("tm"), lax.axis_size("tp")
    rows, width = states.shape
    head_cols = qkv_weight.shape[2]
    heads = head_cols // HD
    seg = rows * tp_count
    lines, chips = tp_count // 2, tm_count // 2
    gw, sw = width // GATHER_CHUNKS, width // SCATTER_CHUNKS
    position = jnp.arange(seg, dtype=jnp.int32)
    bias = jnp.where(position[None, None, :] < segment_lengths[:, None, None], 0.0, -1e30)
    dma = pltpu.SemaphoreType.DMA
    vmem = pl.BlockSpec(memory_space=pltpu.VMEM)
    hbm = pl.BlockSpec(memory_space=pl.ANY)
    g, s = GATHER_CHUNKS, SCATTER_CHUNKS
    return pl.pallas_call(
        functools.partial(kernel, tm_count, tp_count),
        out_shape=jax.ShapeDtypeStruct((rows, width), F32),
        in_specs=[vmem, vmem, hbm, vmem, hbm, vmem],
        out_specs=vmem,
        scratch_shapes=[
            pltpu.VMEM((3, width, head_cols), BF16),
            pltpu.VMEM((head_cols, width), BF16),
            pltpu.VMEM((g, lines, 2, rows, gw), BF16),
            pltpu.VMEM((3, seg, head_cols), F32),
            pltpu.VMEM((heads, seg, HD), BF16),
            pltpu.VMEM((STEPS, tm_count, heads, 2, seg, HD), BF16),
            pltpu.VMEM((seg, head_cols), BF16),
            pltpu.VMEM((heads, seg, HD), F32),
            pltpu.VMEM((heads, seg, HD), F32),
            pltpu.VMEM((heads, seg, HD), F32),
            pltpu.VMEM((s, lines, 2, rows, sw), BF16),
            pltpu.VMEM((s, lines, rows, sw), BF16),
            pltpu.VMEM((s, lines, rows, sw), BF16),
            pltpu.VMEM((s, lines, rows, sw), BF16),
            dma((g,)),
            dma,
            dma((g, lines, 2)),
            dma((g, lines)),
            dma((g, lines)),
            dma((g, lines)),
            dma((STEPS, tm_count, heads)),
            dma((heads,)),
            dma((heads, chips)),
            dma((heads, chips)),
            dma((s,)),
            dma((s,)),
            dma((s, lines)),
            dma((s, lines)),
            dma((s, lines)),
            dma((s, lines)),
        ],
        compiler_params=pltpu.CompilerParams(
            collective_id=0, has_side_effects=True, vmem_limit_bytes=56 * 1024 * 1024
        ),
        cost_estimate=pl.CostEstimate(
            flops=STEPS * 2 * seg * width * head_cols * 4,
            bytes_accessed=width * head_cols * 8,
            transcendentals=STEPS * heads * seg * seg * tm_count,
        ),
    )(
        states,
        norm_gain.reshape(1, width),
        jnp.transpose(qkv_weight, (1, 0, 2)),
        qk_gain,
        out_weight,
        bias.astype(F32),
    )


def solution(mesh):
    return jax.shard_map(
        shards,
        mesh=mesh,
        in_specs=(
            P(("tm", "tp"), None),
            P(),
            P(None, None, "tp"),
            P(None, "tp"),
            P("tp", None),
            P(),
        ),
        out_specs=P(("tm", "tp"), None),
        check_vma=False,
    )
```

```python
import functools
import math

import jax
import jax.numpy as jnp
from jax import lax
from jax.experimental import pallas as pl
from jax.experimental.pallas import tpu as pltpu
from jax.sharding import PartitionSpec as P

HD = 128
STEPS = 2
GATHER_CHUNKS = 6
SCATTER_CHUNKS = 12
LINE_FIRST = 2

eps_norm = 1e-06
step_size = -0.5
BF16 = jnp.bfloat16
F32 = jnp.float32


def remote(src, dst, send_sem, recv_sem, tm, tp):
    return pltpu.make_async_remote_copy(
        src_ref=src,
        dst_ref=dst,
        send_sem=send_sem,
        recv_sem=recv_sem,
        device_id={"tm": tm, "tp": tp},
        device_id_type=pl.DeviceIdType.MESH,
    )


def loop(count, body):
    def step(index, carry):
        body(index)
        return carry

    lax.fori_loop(0, count, step, 0)


def kernel(
    tm_count, tp_count,
    states, gain, w_hbm, qk_gain, wo_hbm, lengths,
    out,
    w, wo, hb, acc, qb, kv, att, run_max, run_acc, pb, yb, ub, db,
    w_sem, wo_sem,
    h_recv, h_part, h_up, h_down,
    kv_recv, kv_sib, kv_chip, kv_fwd,
    y_send, y_recv, u_send, u_recv, d_send, d_recv,
):
    t, p = lax.axis_index("tm"), lax.axis_index("tp")
    lines, chips = tp_count // 2, tm_count // 2
    o, i = p // 2, p % 2
    ch, core = t // 2, t % 2
    partner, above, below = o * 2 + 1 - i, p + 2, p - 2
    sibling = ch * 2 + 1 - core
    has_above, has_below = o < lines - 1, o > 0
    rows, width = states.shape
    seg = rows * tp_count
    head_cols = w.shape[2]
    heads = head_cols // HD
    gw = width // GATHER_CHUNKS
    sw = width // SCATTER_CHUNKS

    def weight_copy(c):
        part = pl.ds(pl.multiple_of(c * gw, gw), gw)
        return pltpu.make_async_copy(w_hbm.at[:, part], w.at[:, part], w_sem.at[c])

    wo_copy = pltpu.make_async_copy(wo_hbm, wo, wo_sem)
    loop(GATHER_CHUNKS, lambda c: weight_copy(c).start())
    wo_copy.start()

    barrier = pltpu.get_barrier_semaphore()

    def greet(tm, tp):
        pl.semaphore_signal(
            barrier, inc=1, device_id={"tm": tm, "tp": tp}, device_id_type=pl.DeviceIdType.MESH
        )

    greet(t, partner)
    greet(sibling, p)

    @pl.when(has_above)
    def _():
        greet(t, above)

    @pl.when(has_below)
    def _():
        greet(t, below)

    for other in range(chips):

        @pl.when(other != ch)
        def _():
            greet(other * 2 + core, p)

    pl.semaphore_wait(
        barrier, 1 + chips + jnp.where(has_above, 1, 0) + jnp.where(has_below, 1, 0)
    )

    out[...] = states[...]

    def h_copy(c, line, side, send_sem, tp):
        ref = hb.at[c, line, side]
        return remote(ref, ref, send_sem.at[c, line, side], h_recv.at[c, line, side], t, tp)

    def h_wait(c, line, side):
        h_copy(c, line, side, h_part, partner).wait_recv()

    def h_both_ways(c, line, side, up, down):
        if up:

            @pl.when(has_above)
            def _():
                h_copy(c, line, side, h_up, above).start()

        if down:

            @pl.when(has_below)
            def _():
                h_copy(c, line, side, h_down, below).start()

    def kv_copy(s, seg_at, h, send_sem, tm):
        ref = kv.at[s, seg_at, h]
        return remote(ref, ref, send_sem, kv_recv.at[s, seg_at, h], tm, p)

    key_at = lax.broadcasted_iota(jnp.int32, (1, seg), 1)
    ones = jnp.ones((seg, HD), BF16)

    def flash(s, h, segments, first):
        scores = [
            lax.dot_general(
                qb[h], kv[s, g, h, 0], (((1,), (1,)), ((), ())), preferred_element_type=F32
            )
            + jnp.where(key_at < lengths[g], 0.0, -1e30)
            for g in segments
        ]
        top = functools.reduce(jnp.maximum, scores)
        top = jnp.max(top, axis=-1, keepdims=True)
        if not first:
            old_top = run_max[h][:, :1]
            top = jnp.maximum(old_top, top)
        update = sum(
            jnp.dot(
                jnp.exp2(part - top).astype(BF16),
                jnp.concatenate([kv[s, g, h, 1], ones], axis=1),
                preferred_element_type=F32,
            )
            for part, g in zip(scores, segments)
        )
        if not first:
            update = update + run_acc[h] * jnp.exp2(old_top - top)
        run_max[h] = jnp.broadcast_to(top, (seg, HD))
        run_acc[h] = update

    def y_copy(c):
        return remote(
            pb.at[c, :, 1 - i], yb.at[c], y_send.at[c], y_recv.at[c], t, partner
        )

    def y_copy_wide(c):
        return remote(
            pb.at[c, o, 1 - i], yb.at[c, 0], y_send.at[c], y_recv.at[c], t, partner
        )

    def rows_of(buffer, c, line, wide):
        return buffer.at[c, line] if wide else buffer.at[c, line, i]

    def u_copy(c, line, wide):
        return remote(
            rows_of(pb, c, line, wide), rows_of(ub, c, line, wide),
            u_send.at[c, line], u_recv.at[c, line], t, above,
        )

    def d_copy(c, line, wide):
        return remote(
            rows_of(pb, c, line, wide), rows_of(db, c, line, wide),
            d_send.at[c, line], d_recv.at[c, line], t, below,
        )

    def step(s):
        square = jnp.zeros((rows, 1), F32)
        for c in range(GATHER_CHUNKS):
            x = out[:, c * gw : (c + 1) * gw]
            square = square + jnp.sum(x * x, axis=-1, keepdims=True)
        scale = lax.rsqrt(square / width + eps_norm)
        last = GATHER_CHUNKS - 1
        for c in [last] + list(range(last)):
            part = slice(c * gw, (c + 1) * gw)
            hb[c, o, i] = (out[:, part] * scale * gain[:, part]).astype(BF16)
            if c < last:
                h_both_ways(c, o, i, True, True)
            h_copy(c, o, i, h_part, partner).start()

        h_both_ways(last, o, i, True, True)
        h_wait(last, o, 1 - i)
        h_both_ways(last, o, 1 - i, True, True)
        for distance in range(1, lines):

            def forward(c):
                @pl.when(o >= distance)
                def _():
                    line = o - distance
                    h_wait(c, line, i)
                    h_both_ways(c, line, i, True, False)
                    h_copy(c, line, i, h_part, partner).start()

                @pl.when(o + distance < lines)
                def _():
                    line = o + distance
                    h_wait(c, line, i)
                    h_both_ways(c, line, i, False, True)
                    h_copy(c, line, i, h_part, partner).start()

            def forward_last():
                for side in (i, 1 - i):

                    @pl.when(o >= distance)
                    def _():
                        h_wait(last, o - distance, side)
                        h_both_ways(last, o - distance, side, True, False)

                    @pl.when(o + distance < lines)
                    def _():
                        h_wait(last, o + distance, side)
                        h_both_ways(last, o + distance, side, False, True)

            loop(last, forward)
            if distance < lines - 1:
                forward_last()

        acc[...] = jnp.zeros_like(acc)

        def project(c):
            @pl.when(c < last)
            def _():
                for line in range(lines):
                    h_wait(c, line, 1 - i)

            @pl.when(c == last)
            def _():
                forward_last()

            @pl.when(s == 0)
            def _():
                weight_copy(c).wait()

            part = pl.ds(pl.multiple_of(c * gw, gw), gw)
            h = hb[c].reshape(seg, gw)
            for j in range(3):
                acc[j] += jnp.dot(h, w[j, part, :], preferred_element_type=F32)

        loop(GATHER_CHUNKS, project)

        for h in range(heads):
            cols = slice(h * HD, (h + 1) * HD)
            k = acc[1, :, cols]
            k_scale = lax.rsqrt(jnp.mean(k * k, axis=-1, keepdims=True) + eps_norm)
            kv[s, t, h, 0] = (k * k_scale * qk_gain[1:2, cols]).astype(BF16)
            kv[s, t, h, 1] = acc[2, :, cols].astype(BF16)
            for other in range(chips):

                @pl.when(other > ch)
                def _():
                    kv_copy(s, t, h, kv_chip.at[h, other], other * 2 + core).start()

            @pl.when(core == 0)
            def _():
                kv_copy(s, t, h, kv_sib.at[h], sibling).start()

        for h in range(heads):
            cols = slice(h * HD, (h + 1) * HD)
            q = acc[0, :, cols]
            q_scale = lax.rsqrt(jnp.mean(q * q, axis=-1, keepdims=True) + eps_norm)
            q_scale = q_scale * (HD ** (-0.5) * math.log2(math.e))
            qb[h] = (q * q_scale * qk_gain[0:1, cols]).astype(BF16)

        @pl.when(core == 0)
        def _():
            for h in range(heads):
                flash(s, h, [t], True)

        @pl.when(core == 1)
        def _():
            for h in range(heads):
                kv_copy(s, t - 1, h, kv_sib.at[h], sibling).wait_recv()
            for h in range(heads):
                flash(s, h, [t, t - 1], True)

        @pl.when(s == 0)
        def _():
            wo_copy.wait()

        def gather_sends(c):
            def one(line):
                h_copy(c, line, i, h_part, partner).wait_send()
                way_sends(c, line, i)

            loop(lines, one)

        def way_sends(c, line, side):
            @pl.when(jnp.logical_and(has_above, line <= o))
            def _():
                h_copy(c, line, side, h_up, above).wait_send()

            @pl.when(jnp.logical_and(has_below, line >= o))
            def _():
                h_copy(c, line, side, h_down, below).wait_send()

        def last_sends(line):
            way_sends(last, line, i)
            way_sends(last, line, 1 - i)

        loop(last, gather_sends)
        h_copy(last, o, i, h_part, partner).wait_send()
        loop(lines, last_sends)

        for group in range(0, heads, 2):
            pair = range(group, min(group + 2, heads))

            def arrived(other):
                @pl.when(other < ch)
                def _():
                    g = other * 2 + core
                    g_passed = other * 2 + 1 - core
                    for h in pair:
                        got = kv_copy(s, g, h, kv_fwd.at[h, other], sibling)
                        got.wait_recv()
                        got.start()
                    for h in pair:
                        kv_copy(s, g_passed, h, kv_fwd.at[h, other], sibling).wait_recv()
                    for h in pair:
                        flash(s, h, [g, g_passed], False)

            loop(chips, arrived)
        for h in range(heads):
            att[:, h * HD : (h + 1) * HD] = (
                run_acc[h][:, :HD] / run_acc[h][:, HD:]
            ).astype(BF16)

        def partial(c):
            part = pl.ds(pl.multiple_of(c * sw, sw), sw)
            product = jnp.dot(att[...], wo[:, part], preferred_element_type=F32)
            pb[c] = product.astype(BF16).reshape(lines, 2, rows, sw)

            @pl.when(c < LINE_FIRST)
            def _():
                start_line(c, True)

            @pl.when(c >= LINE_FIRST)
            def _():
                y_copy(c).start()

        def start_line(c, wide):
            @pl.when(o == 0)
            def _():
                for line in range(1, lines):
                    u_copy(c, line, wide).start()

            @pl.when(o == lines - 1)
            def _():
                for line in range(lines - 1):
                    d_copy(c, line, wide).start()

        loop(SCATTER_CHUNKS, partial)

        def paired(c):
            y_copy(c).wait_recv()
            pb[c, :, i] = (pb[c, :, i].astype(F32) + yb[c].astype(F32)).astype(BF16)
            start_line(c, False)

        def merge(c, line, wide, buffer):
            mine, theirs = rows_of(pb, c, line, wide), rows_of(buffer, c, line, wide)
            mine[...] = (mine[...].astype(F32) + theirs[...].astype(F32)).astype(BF16)

        def hop(c, wide):
            for line in range(1, lines):

                @pl.when(line > o)
                def _():
                    u_copy(c, line, wide).wait_recv()
                    merge(c, line, wide, ub)
                    u_copy(c, line, wide).start()

        def hop_down(c, wide):
            for line in range(lines - 1):

                @pl.when(line < o)
                def _():
                    d_copy(c, line, wide).wait_recv()
                    merge(c, line, wide, db)
                    d_copy(c, line, wide).start()

        def finish(c, wide):
            part = pl.ds(pl.multiple_of(c * sw, sw), sw)

            @pl.when(has_below)
            def _():
                u_copy(c, o, wide).wait_recv()
                merge(c, o, wide, ub)

            @pl.when(has_above)
            def _():
                d_copy(c, o, wide).wait_recv()
                merge(c, o, wide, db)

            if wide:
                y_copy_wide(c).start()
            else:
                out[:, part] += step_size * pb[c, o, i].astype(F32)

        def tick(at):
            @pl.when(jnp.logical_and(at >= LINE_FIRST, at < SCATTER_CHUNKS))
            def _():
                paired(at)

            for k in range(1, lines):
                c = at - k
                for wide, low, high in (
                    (True, 0, LINE_FIRST),
                    (False, LINE_FIRST, SCATTER_CHUNKS),
                ):
                    live = jnp.logical_and(c >= low, c < high)
                    if k < lines - 1:

                        @pl.when(jnp.logical_and(live, o == k))
                        def _():
                            hop(c, wide)

                        @pl.when(jnp.logical_and(live, lines - 1 - o == k))
                        def _():
                            hop_down(c, wide)
                    else:

                        @pl.when(live)
                        def _():
                            finish(c, wide)

        loop(SCATTER_CHUNKS + lines - 1, tick)

        def finish_wide(c):
            part = pl.ds(pl.multiple_of(c * sw, sw), sw)
            y_copy_wide(c).wait_recv()
            out[:, part] += step_size * (pb[c, o, i].astype(F32) + yb[c, 0].astype(F32))

        loop(LINE_FIRST, finish_wide)

        def scatter_sends(c):
            for wide in (True, False):

                @pl.when((c < LINE_FIRST) == wide)
                def _():
                    (y_copy_wide if wide else y_copy)(c).wait_send()

                    def one(line):
                        @pl.when(jnp.logical_and(has_above, line > o))
                        def _():
                            u_copy(c, line, wide).wait_send()

                        @pl.when(jnp.logical_and(has_below, line < o))
                        def _():
                            d_copy(c, line, wide).wait_send()

                    loop(lines, one)

        loop(SCATTER_CHUNKS, scatter_sends)
        for h in range(heads):

            @pl.when(core == 0)
            def _():
                kv_copy(s, t, h, kv_sib.at[h], sibling).wait_send()

            def chip_sends(other):
                @pl.when(other > ch)
                def _():
                    kv_copy(s, t, h, kv_chip.at[h, other], other * 2 + core).wait_send()

                @pl.when(other < ch)
                def _():
                    kv_copy(s, other * 2 + core, h, kv_fwd.at[h, other], sibling).wait_send()

            loop(chips, chip_sends)

    loop(STEPS, step)


def shards(states, norm_gain, qkv_weight, qk_gain, out_weight, segment_lengths):
    tm_count, tp_count = lax.axis_size("tm"), lax.axis_size("tp")
    rows, width = states.shape
    head_cols = qkv_weight.shape[2]
    heads = head_cols // HD
    seg = rows * tp_count
    lines, chips = tp_count // 2, tm_count // 2
    gw, sw = width // GATHER_CHUNKS, width // SCATTER_CHUNKS
    dma = pltpu.SemaphoreType.DMA
    vmem = pl.BlockSpec(memory_space=pltpu.VMEM)
    smem = pl.BlockSpec(memory_space=pltpu.SMEM)
    hbm = pl.BlockSpec(memory_space=pl.ANY)
    g, s = GATHER_CHUNKS, SCATTER_CHUNKS
    return pl.pallas_call(
        functools.partial(kernel, tm_count, tp_count),
        out_shape=jax.ShapeDtypeStruct((rows, width), F32),
        in_specs=[vmem, vmem, hbm, vmem, hbm, smem],
        out_specs=vmem,
        scratch_shapes=[
            pltpu.VMEM((3, width, head_cols), BF16),
            pltpu.VMEM((head_cols, width), BF16),
            pltpu.VMEM((g, lines, 2, rows, gw), BF16),
            pltpu.VMEM((3, seg, head_cols), F32),
            pltpu.VMEM((heads, seg, HD), BF16),
            pltpu.VMEM((STEPS, tm_count, heads, 2, seg, HD), BF16),
            pltpu.VMEM((seg, head_cols), BF16),
            pltpu.VMEM((heads, seg, HD), F32),
            pltpu.VMEM((heads, seg, 2 * HD), F32),
            pltpu.VMEM((s, lines, 2, rows, sw), BF16),
            pltpu.VMEM((s, lines, rows, sw), BF16),
            pltpu.VMEM((s, lines, 2, rows, sw), BF16),
            pltpu.VMEM((s, lines, 2, rows, sw), BF16),
            dma((g,)),
            dma,
            dma((g, lines, 2)),
            dma((g, lines, 2)),
            dma((g, lines, 2)),
            dma((g, lines, 2)),
            dma((STEPS, tm_count, heads)),
            dma((heads,)),
            dma((heads, chips)),
            dma((heads, chips)),
            dma((s,)),
            dma((s,)),
            dma((s, lines)),
            dma((s, lines)),
            dma((s, lines)),
            dma((s, lines)),
        ],
        compiler_params=pltpu.CompilerParams(
            collective_id=0, has_side_effects=True, vmem_limit_bytes=56 * 1024 * 1024
        ),
        cost_estimate=pl.CostEstimate(
            flops=STEPS * 2 * seg * width * head_cols * 4,
            bytes_accessed=width * head_cols * 8,
            transcendentals=STEPS * heads * seg * seg * tm_count,
        ),
    )(
        states,
        norm_gain.reshape(1, width),
        jnp.transpose(qkv_weight, (1, 0, 2)),
        qk_gain,
        out_weight,
        segment_lengths,
    )


def solution(mesh):
    return jax.shard_map(
        shards,
        mesh=mesh,
        in_specs=(
            P(("tm", "tp"), None),
            P(),
            P(None, None, "tp"),
            P(None, "tp"),
            P("tp", None),
            P(),
        ),
        out_specs=P(("tm", "tp"), None),
        check_vma=False,
    )
```

```python
import functools
import math

import jax
import jax.numpy as jnp
from jax import lax
from jax.experimental import pallas as pl
from jax.experimental.pallas import tpu as pltpu
from jax.sharding import PartitionSpec as P

HD = 128
STEPS = 2
GATHER_CHUNKS = 6
SCATTER_CHUNKS = 12
LINE_FIRST = 2

eps_norm = 1e-06
step_size = -0.5
BF16 = jnp.bfloat16
F32 = jnp.float32


def remote(src, dst, send_sem, recv_sem, tm, tp):
    return pltpu.make_async_remote_copy(
        src_ref=src,
        dst_ref=dst,
        send_sem=send_sem,
        recv_sem=recv_sem,
        device_id={"tm": tm, "tp": tp},
        device_id_type=pl.DeviceIdType.MESH,
    )


def loop(count, body):
    def step(index, carry):
        body(index)
        return carry

    lax.fori_loop(0, count, step, 0)


def kernel(
    tm_count, tp_count,
    states, gain, w_hbm, qk_gain, wo_hbm, lengths,
    out,
    w, wo, hb, rb, acc, qb, kv, att, run_max, run_acc, pb, yb, ub, db,
    w_sem, wo_sem,
    h_recv, h_part, h_up, h_down,
    r_recv, r_part, r_up, r_down,
    kv_recv, kv_sib, kv_chip, kv_fwd,
    y_send, y_recv, u_send, u_recv, d_send, d_recv,
):
    t, p = lax.axis_index("tm"), lax.axis_index("tp")
    lines, chips = tp_count // 2, tm_count // 2
    o, i = p // 2, p % 2
    ch, core = t // 2, t % 2
    partner, above, below = o * 2 + 1 - i, p + 2, p - 2
    sibling = ch * 2 + 1 - core
    has_above, has_below = o < lines - 1, o > 0
    rows, width = states.shape
    seg = rows * tp_count
    head_cols = w.shape[2]
    heads = head_cols // HD
    gw = width // GATHER_CHUNKS
    sw = width // SCATTER_CHUNKS
    per_gather = SCATTER_CHUNKS // GATHER_CHUNKS
    both = 0

    def weight_copy(c):
        part = pl.ds(pl.multiple_of(c * gw, gw), gw)
        return pltpu.make_async_copy(w_hbm.at[:, part], w.at[:, part], w_sem.at[c])

    wo_copy = pltpu.make_async_copy(wo_hbm, wo, wo_sem)
    loop(GATHER_CHUNKS, lambda c: weight_copy(c).start())
    wo_copy.start()

    barrier = pltpu.get_barrier_semaphore()

    def greet(tm, tp):
        pl.semaphore_signal(
            barrier, inc=1, device_id={"tm": tm, "tp": tp}, device_id_type=pl.DeviceIdType.MESH
        )

    greet(t, partner)
    greet(sibling, p)

    @pl.when(has_above)
    def _():
        greet(t, above)

    @pl.when(has_below)
    def _():
        greet(t, below)

    for other in range(chips):

        @pl.when(other != ch)
        def _():
            greet(other * 2 + core, p)

    out[...] = states[...]

    def prepare(c):
        part = pl.ds(pl.multiple_of(c * gw, gw), gw)
        hb[c, o, i] = (out[:, part] * gain[:, part]).astype(BF16)

    on_diagonal = lax.broadcasted_iota(
        jnp.int32, (rows, HD), 0
    ) == lax.broadcasted_iota(jnp.int32, (rows, HD), 1)

    def prepare_scale():
        square = jnp.zeros((rows, 1), F32)
        for c in range(GATHER_CHUNKS):
            x = out[:, c * gw : (c + 1) * gw]
            square = square + jnp.sum(x * x, axis=-1, keepdims=True)
        scale = lax.rsqrt(square / width + eps_norm)
        laid = jnp.sum(jnp.where(on_diagonal, scale, 0.0), axis=0, keepdims=True)
        rb[o, i] = jnp.broadcast_to(laid, (8, HD))

    def scale_column(line, side):
        laid = jnp.broadcast_to(rb[line, side][0:1], (rows, HD))
        return jnp.sum(jnp.where(on_diagonal, laid, 0.0), axis=-1, keepdims=True)

    loop(GATHER_CHUNKS, prepare)
    prepare_scale()

    pl.semaphore_wait(
        barrier, 1 + chips + jnp.where(has_above, 1, 0) + jnp.where(has_below, 1, 0)
    )


    def h_copy(c, line, side, send_sem, tp):
        ref = hb.at[c, line, side]
        return remote(ref, ref, send_sem.at[c, line, side], h_recv.at[c, line, side], t, tp)

    def h_wait(c, line, side):
        h_copy(c, line, side, h_part, partner).wait_recv()

    def h_both_ways(c, line, side, up, down):
        if up:

            @pl.when(has_above)
            def _():
                h_copy(c, line, side, h_up, above).start()

        if down:

            @pl.when(has_below)
            def _():
                h_copy(c, line, side, h_down, below).start()

    def r_copy(line, side, send_sem, tp):
        ref = rb.at[line, side]
        return remote(ref, ref, send_sem.at[line], r_recv.at[line, side], t, tp)

    def r_forward(line, up, down):
        if up:

            @pl.when(has_above)
            def _():
                r_copy(line, i, r_up, above).start()

        if down:

            @pl.when(has_below)
            def _():
                r_copy(line, i, r_down, below).start()

        r_copy(line, i, r_part, partner).start()

    def send_own(c):
        h_both_ways(c, o, i, True, True)
        h_copy(c, o, i, h_part, partner).start()

    def kv_copy(s, seg_at, h, send_sem, tm):
        ref = kv.at[s, seg_at, h]
        return remote(ref, ref, send_sem, kv_recv.at[s, seg_at, h], tm, p)

    key_at = lax.broadcasted_iota(jnp.int32, (1, seg), 1)
    ones = jnp.ones((seg, HD), BF16)

    def flash(s, h, segments, first):
        scores = [
            lax.dot_general(
                qb[h], kv[s, g, h, 0], (((1,), (1,)), ((), ())), preferred_element_type=F32
            )
            + jnp.where(key_at < lengths[g], 0.0, -1e30)
            for g in segments
        ]
        top = functools.reduce(jnp.maximum, scores)
        top = jnp.max(top, axis=-1, keepdims=True)
        if not first:
            old_top = run_max[h][:, :1]
            top = jnp.maximum(old_top, top)
        update = sum(
            jnp.dot(
                jnp.exp2(part - top).astype(BF16),
                jnp.concatenate([kv[s, g, h, 1], ones], axis=1),
                preferred_element_type=F32,
            )
            for part, g in zip(scores, segments)
        )
        if not first:
            update = update + run_acc[h] * jnp.exp2(old_top - top)
        run_max[h] = jnp.broadcast_to(top, (seg, HD))
        run_acc[h] = update

    def y_copy(c):
        return remote(
            pb.at[c, :, 1 - i], yb.at[c], y_send.at[c], y_recv.at[c], t, partner
        )

    def y_copy_wide(c):
        return remote(
            pb.at[c, o, 1 - i], yb.at[c, 0], y_send.at[c], y_recv.at[c], t, partner
        )

    def rows_of(buffer, c, line, wide):
        return buffer.at[c, line] if wide else buffer.at[c, line, i]

    def u_copy(c, line, wide):
        return remote(
            rows_of(pb, c, line, wide), rows_of(ub, c, line, wide),
            u_send.at[c, line], u_recv.at[c, line], t, above,
        )

    def d_copy(c, line, wide):
        return remote(
            rows_of(pb, c, line, wide), rows_of(db, c, line, wide),
            d_send.at[c, line], d_recv.at[c, line], t, below,
        )

    def step(s):
        h_both_ways(both, o, i, True, True)
        h_wait(both, o, 1 - i)
        h_both_ways(both, o, 1 - i, True, True)
        acc[...] = jnp.zeros_like(acc)
        for distance in range(1, lines):

            def forward(c):
                @pl.when(o >= distance)
                def _():
                    line = o - distance
                    h_wait(c, line, i)
                    h_both_ways(c, line, i, True, False)
                    h_copy(c, line, i, h_part, partner).start()

                @pl.when(o + distance < lines)
                def _():
                    line = o + distance
                    h_wait(c, line, i)
                    h_both_ways(c, line, i, False, True)
                    h_copy(c, line, i, h_part, partner).start()

            def forward_both():
                for side in (i, 1 - i):

                    @pl.when(o >= distance)
                    def _():
                        h_wait(both, o - distance, side)
                        h_both_ways(both, o - distance, side, True, False)

                    @pl.when(o + distance < lines)
                    def _():
                        h_wait(both, o + distance, side)
                        h_both_ways(both, o + distance, side, False, True)

            def forward_scale():
                @pl.when(o >= distance)
                def _():
                    r_copy(o - distance, i, r_part, partner).wait_recv()
                    r_forward(o - distance, True, False)

                @pl.when(o + distance < lines)
                def _():
                    r_copy(o + distance, i, r_part, partner).wait_recv()
                    r_forward(o + distance, False, True)

            if distance < lines - 1:
                loop(GATHER_CHUNKS - 1, lambda c: forward(c + 1))
                forward_scale()
                forward_both()

        def project(c):
            @pl.when(c != both)
            def _():
                for line in range(lines):
                    h_wait(c, line, 1 - i)

            @pl.when(c == both)
            def _():
                forward_scale()
                forward_both()

            @pl.when(s == 0)
            def _():
                weight_copy(c).wait()

            part = pl.ds(pl.multiple_of(c * gw, gw), gw)
            h = hb[c].reshape(seg, gw)
            for j in range(3):
                acc[j] += jnp.dot(h, w[j, part, :], preferred_element_type=F32)

        def farthest(at):
            @pl.when(at < GATHER_CHUNKS - 1)
            def _():
                forward(at + 1)

            @pl.when(at >= 2)
            def _():
                project(jnp.where(at == GATHER_CHUNKS + 1, both, at - 1))

        loop(GATHER_CHUNKS + 2, farthest)
        for line in range(lines):
            r_copy(line, 1 - i, r_part, partner).wait_recv()
        for line in range(lines):
            for side in range(2):
                here = pl.ds((line * 2 + side) * rows, rows)
                acc[:, here, :] = acc[:, here, :] * scale_column(line, side)

        for h in range(heads):
            cols = slice(h * HD, (h + 1) * HD)
            k = acc[1, :, cols]
            k_scale = lax.rsqrt(jnp.mean(k * k, axis=-1, keepdims=True) + eps_norm)
            kv[s, t, h, 0] = (k * k_scale * qk_gain[1:2, cols]).astype(BF16)
            kv[s, t, h, 1] = acc[2, :, cols].astype(BF16)
            for other in range(chips):

                @pl.when(other > ch)
                def _():
                    kv_copy(s, t, h, kv_chip.at[h, other], other * 2 + core).start()

            @pl.when(core == 0)
            def _():
                kv_copy(s, t, h, kv_sib.at[h], sibling).start()

        for h in range(heads):
            cols = slice(h * HD, (h + 1) * HD)
            q = acc[0, :, cols]
            q_scale = lax.rsqrt(jnp.mean(q * q, axis=-1, keepdims=True) + eps_norm)
            q_scale = q_scale * (HD ** (-0.5) * math.log2(math.e))
            qb[h] = (q * q_scale * qk_gain[0:1, cols]).astype(BF16)

        @pl.when(core == 0)
        def _():
            for h in range(heads):
                flash(s, h, [t], True)

        @pl.when(core == 1)
        def _():
            for h in range(heads):
                kv_copy(s, t - 1, h, kv_sib.at[h], sibling).wait_recv()
            for h in range(heads):
                flash(s, h, [t, t - 1], True)

        @pl.when(s == 0)
        def _():
            wo_copy.wait()

        def gather_sends(c):
            def one(line):
                h_copy(c, line, i, h_part, partner).wait_send()
                way_sends(c, line, i)

            loop(lines, one)

        def scale_sends(line):
            r_copy(line, i, r_part, partner).wait_send()

            @pl.when(jnp.logical_and(has_above, line <= o))
            def _():
                r_copy(line, i, r_up, above).wait_send()

            @pl.when(jnp.logical_and(has_below, line >= o))
            def _():
                r_copy(line, i, r_down, below).wait_send()

        def way_sends(c, line, side):
            @pl.when(jnp.logical_and(has_above, line <= o))
            def _():
                h_copy(c, line, side, h_up, above).wait_send()

            @pl.when(jnp.logical_and(has_below, line >= o))
            def _():
                h_copy(c, line, side, h_down, below).wait_send()

        def both_sends(line):
            way_sends(both, line, i)
            way_sends(both, line, 1 - i)

        loop(GATHER_CHUNKS - 1, lambda c: gather_sends(c + 1))
        h_copy(both, o, i, h_part, partner).wait_send()
        loop(lines, both_sends)
        loop(lines, scale_sends)

        for group in range(0, heads, 2):
            pair = range(group, min(group + 2, heads))

            def arrived(other):
                @pl.when(other < ch)
                def _():
                    g = other * 2 + core
                    g_passed = other * 2 + 1 - core
                    for h in pair:
                        got = kv_copy(s, g, h, kv_fwd.at[h, other], sibling)
                        got.wait_recv()
                        got.start()
                    for h in pair:
                        kv_copy(s, g_passed, h, kv_fwd.at[h, other], sibling).wait_recv()
                    for h in pair:
                        flash(s, h, [g, g_passed], False)

            loop(chips, arrived)
        for h in range(heads):
            att[:, h * HD : (h + 1) * HD] = (
                run_acc[h][:, :HD] / run_acc[h][:, HD:]
            ).astype(BF16)

        def partial(c):
            part = pl.ds(pl.multiple_of(c * sw, sw), sw)
            product = jnp.dot(att[...], wo[:, part], preferred_element_type=F32)
            pb[c] = product.astype(BF16).reshape(lines, 2, rows, sw)

            @pl.when(c < LINE_FIRST)
            def _():
                start_line(c, True)

            @pl.when(c >= LINE_FIRST)
            def _():
                y_copy(c).start()

        def start_line(c, wide):
            @pl.when(o == 0)
            def _():
                for line in range(lines - 1, 0, -1):
                    u_copy(c, line, wide).start()

            @pl.when(o == lines - 1)
            def _():
                for line in range(lines - 1):
                    d_copy(c, line, wide).start()

        loop(SCATTER_CHUNKS, partial)

        def paired(c):
            y_copy(c).wait_recv()
            pb[c, :, i] = (pb[c, :, i].astype(F32) + yb[c].astype(F32)).astype(BF16)
            start_line(c, False)

        def merge(c, line, wide, buffer):
            mine, theirs = rows_of(pb, c, line, wide), rows_of(buffer, c, line, wide)
            mine[...] = (mine[...].astype(F32) + theirs[...].astype(F32)).astype(BF16)

        def hop(c, wide):
            for line in range(lines - 1, 0, -1):

                @pl.when(line > o)
                def _():
                    u_copy(c, line, wide).wait_recv()
                    merge(c, line, wide, ub)
                    u_copy(c, line, wide).start()

        def hop_down(c, wide):
            for line in range(lines - 1):

                @pl.when(line < o)
                def _():
                    d_copy(c, line, wide).wait_recv()
                    merge(c, line, wide, db)
                    d_copy(c, line, wide).start()

        def finish(c, wide):
            part = pl.ds(pl.multiple_of(c * sw, sw), sw)

            @pl.when(has_below)
            def _():
                u_copy(c, o, wide).wait_recv()
                merge(c, o, wide, ub)

            @pl.when(has_above)
            def _():
                d_copy(c, o, wide).wait_recv()
                merge(c, o, wide, db)

            if wide:
                y_copy_wide(c).start()
            else:
                out[:, part] += step_size * pb[c, o, i].astype(F32)

                @pl.when(jnp.logical_and(s < STEPS - 1, c % per_gather == per_gather - 1))
                def _():
                    prepare(c // per_gather)
                    send_own(c // per_gather)

        def tick(at):
            @pl.when(jnp.logical_and(at >= LINE_FIRST, at < SCATTER_CHUNKS))
            def _():
                paired(at)

            for k in range(1, lines):
                c = at - k
                for wide, low, high in (
                    (True, 0, LINE_FIRST),
                    (False, LINE_FIRST, SCATTER_CHUNKS),
                ):
                    live = jnp.logical_and(c >= low, c < high)
                    if k < lines - 1:

                        @pl.when(jnp.logical_and(live, o == k))
                        def _():
                            hop(c, wide)

                        @pl.when(jnp.logical_and(live, lines - 1 - o == k))
                        def _():
                            hop_down(c, wide)
                    else:

                        @pl.when(live)
                        def _():
                            finish(c, wide)

        def finish_wide(c):
            part = pl.ds(pl.multiple_of(c * sw, sw), sw)
            y_copy_wide(c).wait_recv()
            out[:, part] += step_size * (pb[c, o, i].astype(F32) + yb[c, 0].astype(F32))

        def tick_all(at):
            tick(at)

            @pl.when(at == SCATTER_CHUNKS)
            def _():
                loop(LINE_FIRST, finish_wide)

                @pl.when(s < STEPS - 1)
                def _():
                    prepare(both)
                    h_copy(both, o, i, h_part, partner).start()

        loop(SCATTER_CHUNKS + lines - 1, tick_all)

        @pl.when(s < STEPS - 1)
        def _():
            prepare_scale()
            r_forward(o, True, True)

        def scatter_sends(c):
            for wide in (True, False):

                @pl.when((c < LINE_FIRST) == wide)
                def _():
                    (y_copy_wide if wide else y_copy)(c).wait_send()

                    def one(line):
                        @pl.when(jnp.logical_and(has_above, line > o))
                        def _():
                            u_copy(c, line, wide).wait_send()

                        @pl.when(jnp.logical_and(has_below, line < o))
                        def _():
                            d_copy(c, line, wide).wait_send()

                    loop(lines, one)

        loop(SCATTER_CHUNKS, scatter_sends)
        for h in range(heads):

            @pl.when(core == 0)
            def _():
                kv_copy(s, t, h, kv_sib.at[h], sibling).wait_send()

            def chip_sends(other):
                @pl.when(other > ch)
                def _():
                    kv_copy(s, t, h, kv_chip.at[h, other], other * 2 + core).wait_send()

                @pl.when(other < ch)
                def _():
                    kv_copy(s, other * 2 + core, h, kv_fwd.at[h, other], sibling).wait_send()

            loop(chips, chip_sends)

    h_copy(both, o, i, h_part, partner).start()
    for c in range(1, GATHER_CHUNKS):
        send_own(c)
    r_forward(o, True, True)
    loop(STEPS, step)


def shards(states, norm_gain, qkv_weight, qk_gain, out_weight, segment_lengths):
    tm_count, tp_count = lax.axis_size("tm"), lax.axis_size("tp")
    rows, width = states.shape
    head_cols = qkv_weight.shape[2]
    heads = head_cols // HD
    seg = rows * tp_count
    lines, chips = tp_count // 2, tm_count // 2
    gw, sw = width // GATHER_CHUNKS, width // SCATTER_CHUNKS
    dma = pltpu.SemaphoreType.DMA
    vmem = pl.BlockSpec(memory_space=pltpu.VMEM)
    smem = pl.BlockSpec(memory_space=pltpu.SMEM)
    hbm = pl.BlockSpec(memory_space=pl.ANY)
    g, s = GATHER_CHUNKS, SCATTER_CHUNKS
    return pl.pallas_call(
        functools.partial(kernel, tm_count, tp_count),
        out_shape=jax.ShapeDtypeStruct((rows, width), F32),
        in_specs=[vmem, vmem, hbm, vmem, hbm, smem],
        out_specs=vmem,
        scratch_shapes=[
            pltpu.VMEM((3, width, head_cols), BF16),
            pltpu.VMEM((head_cols, width), BF16),
            pltpu.VMEM((g, lines, 2, rows, gw), BF16),
            pltpu.VMEM((lines, 2, 8, HD), F32),
            pltpu.VMEM((3, seg, head_cols), F32),
            pltpu.VMEM((heads, seg, HD), BF16),
            pltpu.VMEM((STEPS, tm_count, heads, 2, seg, HD), BF16),
            pltpu.VMEM((seg, head_cols), BF16),
            pltpu.VMEM((heads, seg, HD), F32),
            pltpu.VMEM((heads, seg, 2 * HD), F32),
            pltpu.VMEM((s, lines, 2, rows, sw), BF16),
            pltpu.VMEM((s, lines, rows, sw), BF16),
            pltpu.VMEM((s, lines, 2, rows, sw), BF16),
            pltpu.VMEM((s, lines, 2, rows, sw), BF16),
            dma((g,)),
            dma,
            dma((g, lines, 2)),
            dma((g, lines, 2)),
            dma((g, lines, 2)),
            dma((g, lines, 2)),
            dma((lines, 2)),
            dma((lines,)),
            dma((lines,)),
            dma((lines,)),
            dma((STEPS, tm_count, heads)),
            dma((heads,)),
            dma((heads, chips)),
            dma((heads, chips)),
            dma((s,)),
            dma((s,)),
            dma((s, lines)),
            dma((s, lines)),
            dma((s, lines)),
            dma((s, lines)),
        ],
        compiler_params=pltpu.CompilerParams(
            collective_id=0, has_side_effects=True, vmem_limit_bytes=56 * 1024 * 1024
        ),
        cost_estimate=pl.CostEstimate(
            flops=STEPS * 2 * seg * width * head_cols * 4,
            bytes_accessed=width * head_cols * 8,
            transcendentals=STEPS * heads * seg * seg * tm_count,
        ),
    )(
        states,
        norm_gain.reshape(1, width),
        jnp.transpose(qkv_weight, (1, 0, 2)),
        qk_gain,
        out_weight,
        segment_lengths,
    )


def solution(mesh):
    return jax.shard_map(
        shards,
        mesh=mesh,
        in_specs=(
            P(("tm", "tp"), None),
            P(),
            P(None, None, "tp"),
            P(None, "tp"),
            P("tp", None),
            P(),
        ),
        out_specs=P(("tm", "tp"), None),
        check_vma=False,
    )
```

```python
import functools
import math

import jax
import jax.numpy as jnp
from jax import lax
from jax.experimental import pallas as pl
from jax.experimental.pallas import tpu as pltpu
from jax.sharding import PartitionSpec as P

HD = 128
STEPS = 2
GATHER_CHUNKS = 6
GROUP = 3
SCATTER_CHUNKS = 12
LINE_FIRST = 2

eps_norm = 1e-06
step_size = -0.5
BF16 = jnp.bfloat16
F32 = jnp.float32


def remote(src, dst, send_sem, recv_sem, tm, tp):
    return pltpu.make_async_remote_copy(
        src_ref=src,
        dst_ref=dst,
        send_sem=send_sem,
        recv_sem=recv_sem,
        device_id={"tm": tm, "tp": tp},
        device_id_type=pl.DeviceIdType.MESH,
    )


def halves_of(rows):
    return 2 if rows % 32 == 0 else 1


def loop(count, body):
    def step(index, carry):
        body(index)
        return carry

    lax.fori_loop(0, count, step, 0)


def kernel(
    tm_count, tp_count,
    states, gain, w_hbm, qk_gain, wo_hbm, lengths,
    out,
    w, wo, hb, rb, acc, qb, kv, att, run_max, run_acc, pb, yb, ub, db,
    w_sem, wo_sem,
    h_recv, h_part, h_up, h_down,
    r_recv, r_part, r_up, r_down,
    kv_recv, kv_sib, kv_chip, kv_fwd,
    y_send, y_recv, u_send, u_recv, d_send, d_recv,
):
    t, p = lax.axis_index("tm"), lax.axis_index("tp")
    lines, chips = tp_count // 2, tm_count // 2
    o, i = p // 2, p % 2
    ch, core = t // 2, t % 2
    partner, above, below = o * 2 + 1 - i, p + 2, p - 2
    sibling = ch * 2 + 1 - core
    has_above, has_below = o < lines - 1, o > 0
    rows, width = states.shape
    seg = rows * tp_count
    head_cols = w.shape[2]
    heads = head_cols // HD
    halves = halves_of(rows)
    rh, sh = rows // halves, seg // halves
    gw = width * halves // GATHER_CHUNKS
    sw = width // SCATTER_CHUNKS
    parts = width // gw
    per_gather = gw // sw
    both = GROUP

    def weight_copy(c):
        part = pl.ds(pl.multiple_of(c * gw, gw), gw)
        return pltpu.make_async_copy(w_hbm.at[:, part], w.at[:, part], w_sem.at[c])

    wo_copy = pltpu.make_async_copy(wo_hbm, wo, wo_sem)
    loop(parts, lambda c: weight_copy(c).start())
    wo_copy.start()

    barrier = pltpu.get_barrier_semaphore()

    def greet(tm, tp):
        pl.semaphore_signal(
            barrier, inc=1, device_id={"tm": tm, "tp": tp}, device_id_type=pl.DeviceIdType.MESH
        )

    greet(t, partner)
    greet(sibling, p)

    @pl.when(has_above)
    def _():
        greet(t, above)

    @pl.when(has_below)
    def _():
        greet(t, below)

    for other in range(chips):

        @pl.when(other != ch)
        def _():
            greet(other * 2 + core, p)

    out[...] = states[...]

    def prepare(c):
        part = pl.ds(pl.multiple_of(c % parts * gw, gw), gw)
        here = pl.ds(pl.multiple_of(c // parts * rh, rh), rh)
        hb[c, o, i] = (out[here, part] * gain[:, part]).astype(BF16)

    on_diagonal = lax.broadcasted_iota(
        jnp.int32, (rows, HD), 0
    ) == lax.broadcasted_iota(jnp.int32, (rows, HD), 1)

    def prepare_scale():
        square = jnp.zeros((rows, 1), F32)
        for c in range(SCATTER_CHUNKS):
            x = out[:, c * sw : (c + 1) * sw]
            square = square + jnp.sum(x * x, axis=-1, keepdims=True)
        scale = lax.rsqrt(square / width + eps_norm)
        laid = jnp.sum(jnp.where(on_diagonal, scale, 0.0), axis=0, keepdims=True)
        rb[o, i] = jnp.broadcast_to(laid, (8, HD))

    def scale_column(line, side):
        laid = jnp.broadcast_to(rb[line, side][0:1], (rows, HD))
        return jnp.sum(jnp.where(on_diagonal, laid, 0.0), axis=-1, keepdims=True)

    loop(GATHER_CHUNKS, prepare)
    prepare_scale()

    pl.semaphore_wait(
        barrier, 1 + chips + jnp.where(has_above, 1, 0) + jnp.where(has_below, 1, 0)
    )


    def h_copy(c, line, side, send_sem, tp):
        ref = hb.at[c, line, side]
        return remote(ref, ref, send_sem.at[c, line, side], h_recv.at[c, line, side], t, tp)

    def h_wait(c, line, side):
        h_copy(c, line, side, h_part, partner).wait_recv()

    def h_both_ways(c, line, side, up, down):
        if up:

            @pl.when(has_above)
            def _():
                h_copy(c, line, side, h_up, above).start()

        if down:

            @pl.when(has_below)
            def _():
                h_copy(c, line, side, h_down, below).start()

    def r_copy(line, side, send_sem, tp):
        ref = rb.at[line, side]
        return remote(ref, ref, send_sem.at[line], r_recv.at[line, side], t, tp)

    def r_forward(line, up, down):
        if up:

            @pl.when(has_above)
            def _():
                r_copy(line, i, r_up, above).start()

        if down:

            @pl.when(has_below)
            def _():
                r_copy(line, i, r_down, below).start()

        r_copy(line, i, r_part, partner).start()

    def send_own(c):
        h_both_ways(c, o, i, True, True)
        h_copy(c, o, i, h_part, partner).start()

    def kv_copy(s, seg_at, h, half, send_sem, tm):
        ref = kv.at[s, seg_at, h, half]
        return remote(ref, ref, send_sem.at[half], kv_recv.at[s, seg_at, h, half], tm, p)

    key_at = lax.broadcasted_iota(jnp.int32, (1, seg), 1)
    key_at = key_at % sh // rh * rows + key_at // sh * rh + key_at % rh
    ones = jnp.ones((seg, HD), BF16)

    def flash(s, h, segments, first):
        scores = [
            lax.dot_general(
                qb[h], kv[s, g, h, :, 0].reshape(seg, HD), (((1,), (1,)), ((), ())), preferred_element_type=F32
            )
            + jnp.where(key_at < lengths[g], 0.0, -1e30)
            for g in segments
        ]
        top = functools.reduce(jnp.maximum, scores)
        top = jnp.max(top, axis=-1, keepdims=True)
        if not first:
            old_top = run_max[h][:, :1]
            top = jnp.maximum(old_top, top)
        update = sum(
            jnp.dot(
                jnp.exp2(part - top).astype(BF16),
                jnp.concatenate([kv[s, g, h, :, 1].reshape(seg, HD), ones], axis=1),
                preferred_element_type=F32,
            )
            for part, g in zip(scores, segments)
        )
        if not first:
            update = update + run_acc[h] * jnp.exp2(old_top - top)
        run_max[h] = jnp.broadcast_to(top, (seg, HD))
        run_acc[h] = update

    def y_copy(c):
        return remote(
            pb.at[c, :, 1 - i], yb.at[c], y_send.at[c], y_recv.at[c], t, partner
        )

    def y_copy_wide(c):
        return remote(
            pb.at[c, o, 1 - i], yb.at[c, 0], y_send.at[c], y_recv.at[c], t, partner
        )

    def rows_of(buffer, c, line, wide):
        return buffer.at[c, line] if wide else buffer.at[c, line, i]

    def u_copy(c, line, wide):
        return remote(
            rows_of(pb, c, line, wide), rows_of(ub, c, line, wide),
            u_send.at[c, line], u_recv.at[c, line], t, above,
        )

    def d_copy(c, line, wide):
        return remote(
            rows_of(pb, c, line, wide), rows_of(db, c, line, wide),
            d_send.at[c, line], d_recv.at[c, line], t, below,
        )

    def step(s):
        def forward(c, distance):
            @pl.when(o >= distance)
            def _():
                line = o - distance
                h_wait(c, line, i)
                h_both_ways(c, line, i, True, False)
                h_copy(c, line, i, h_part, partner).start()

            @pl.when(o + distance < lines)
            def _():
                line = o + distance
                h_wait(c, line, i)
                h_both_ways(c, line, i, False, True)
                h_copy(c, line, i, h_part, partner).start()

        def forward_both(distance):
            for side in (i, 1 - i):

                @pl.when(o >= distance)
                def _():
                    h_wait(both, o - distance, side)
                    h_both_ways(both, o - distance, side, True, False)

                @pl.when(o + distance < lines)
                def _():
                    h_wait(both, o + distance, side)
                    h_both_ways(both, o + distance, side, False, True)

        def forward_scale(distance):
            @pl.when(o >= distance)
            def _():
                r_copy(o - distance, i, r_part, partner).wait_recv()
                r_forward(o - distance, True, False)

            @pl.when(o + distance < lines)
            def _():
                r_copy(o + distance, i, r_part, partner).wait_recv()
                r_forward(o + distance, False, True)

        def project(c):
            @pl.when(c != both)
            def _():
                for line in range(lines):
                    h_wait(c, line, 1 - i)

            @pl.when(jnp.logical_and(s == 0, c < parts))
            def _():
                weight_copy(c).wait()

            part = pl.ds(pl.multiple_of(c % parts * gw, gw), gw)
            h = hb[c].reshape(sh, gw)
            for j in range(3):
                acc[c // parts, j] += jnp.dot(h, w[j, part, :], preferred_element_type=F32)

        def scales(half):
            return jnp.concatenate(
                [
                    scale_column(line, side)[half * rh : (half + 1) * rh]
                    for line in range(lines)
                    for side in range(2)
                ],
                axis=0,
            )

        def emit_keys(half):
            scale = scales(half)
            for h in range(heads):
                cols = slice(h * HD, (h + 1) * HD)
                k = acc[half, 1, :, cols] * scale
                k_scale = lax.rsqrt(jnp.mean(k * k, axis=-1, keepdims=True) + eps_norm)
                kv[s, t, h, half, 0] = (k * k_scale * qk_gain[1:2, cols]).astype(BF16)
                kv[s, t, h, half, 1] = (acc[half, 2, :, cols] * scale).astype(BF16)
                for other in range(chips):

                    @pl.when(other > ch)
                    def _():
                        kv_copy(
                            s, t, h, half, kv_chip.at[h, other], other * 2 + core
                        ).start()

                @pl.when(core == 0)
                def _():
                    kv_copy(s, t, h, half, kv_sib.at[h], sibling).start()

        def emit_queries(half):
            scale = scales(half)
            for h in range(heads):
                cols = slice(h * HD, (h + 1) * HD)
                q = acc[half, 0, :, cols] * scale
                q_scale = lax.rsqrt(jnp.mean(q * q, axis=-1, keepdims=True) + eps_norm)
                q_scale = q_scale * (HD ** (-0.5) * math.log2(math.e))
                qb[h, half * sh : (half + 1) * sh] = (
                    q * q_scale * qk_gain[0:1, cols]
                ).astype(BF16)

        rest = GATHER_CHUNKS - GROUP - 1
        acc[...] = jnp.zeros_like(acc)
        for distance in range(1, lines - 1):
            loop(GROUP, lambda c: forward(c, distance))
            forward_scale(distance)
        loop(rest, lambda c: h_both_ways(c + both + 1, o, i, True, True))
        h_both_ways(both, o, i, True, True)
        h_wait(both, o, 1 - i)
        h_both_ways(both, o, 1 - i, True, True)
        loop(GROUP, lambda c: forward(c, lines - 1))
        forward_scale(lines - 1)
        loop(rest, lambda c: h_copy(c + both + 1, o, i, h_part, partner).start())
        for line in range(lines):
            r_copy(line, 1 - i, r_part, partner).wait_recv()

        for distance in range(1, lines - 1):

            def second(c):
                forward(c + both + 1, distance)
                if distance == 1:
                    project(c)

            loop(rest, second)
            forward_both(distance)
            if distance == 1:
                loop(GROUP - rest, lambda c: project(c + rest))
                if halves == 2:
                    emit_keys(0)
            elif distance == 2 and halves == 2:
                emit_queries(0)

        loop(rest, lambda c: forward(c + both + 1, lines - 1))

        def final(c):
            @pl.when(c == rest)
            def _():
                forward_both(lines - 1)

            project(jnp.where(c == rest, both, c + both + 1))

        loop(rest + 1, final)
        emit_keys(halves - 1)
        emit_queries(halves - 1)

        @pl.when(core == 0)
        def _():
            for h in range(heads):
                flash(s, h, [t], True)

        @pl.when(core == 1)
        def _():
            for h in range(heads):
                for half in range(halves):
                    kv_copy(s, t - 1, h, half, kv_sib.at[h], sibling).wait_recv()
            for h in range(heads):
                flash(s, h, [t, t - 1], True)

        @pl.when(s == 0)
        def _():
            wo_copy.wait()

        def gather_sends(c):
            def one(line):
                h_copy(c, line, i, h_part, partner).wait_send()
                way_sends(c, line, i)

            loop(lines, one)

        def scale_sends(line):
            r_copy(line, i, r_part, partner).wait_send()

            @pl.when(jnp.logical_and(has_above, line <= o))
            def _():
                r_copy(line, i, r_up, above).wait_send()

            @pl.when(jnp.logical_and(has_below, line >= o))
            def _():
                r_copy(line, i, r_down, below).wait_send()

        def way_sends(c, line, side):
            @pl.when(jnp.logical_and(has_above, line <= o))
            def _():
                h_copy(c, line, side, h_up, above).wait_send()

            @pl.when(jnp.logical_and(has_below, line >= o))
            def _():
                h_copy(c, line, side, h_down, below).wait_send()

        def both_sends(line):
            way_sends(both, line, i)
            way_sends(both, line, 1 - i)

        def chunk_sends(c):
            @pl.when(c != both)
            def _():
                gather_sends(c)

        loop(GATHER_CHUNKS, chunk_sends)
        h_copy(both, o, i, h_part, partner).wait_send()
        loop(lines, both_sends)
        loop(lines, scale_sends)

        for group in range(0, heads, 2):
            pair = range(group, min(group + 2, heads))

            def arrived(other):
                @pl.when(other < ch)
                def _():
                    g = other * 2 + core
                    g_passed = other * 2 + 1 - core
                    for h in pair:
                        for half in range(halves):
                            got = kv_copy(s, g, h, half, kv_fwd.at[h, other], sibling)
                            got.wait_recv()
                            got.start()
                    for h in pair:
                        for half in range(halves):
                            kv_copy(
                                s, g_passed, h, half, kv_fwd.at[h, other], sibling
                            ).wait_recv()
                    for h in pair:
                        flash(s, h, [g, g_passed], False)

            loop(chips, arrived)
        for h in range(heads):
            att[:, h * HD : (h + 1) * HD] = (
                run_acc[h][:, :HD] / run_acc[h][:, HD:]
            ).astype(BF16)

        def partial(c):
            part = pl.ds(pl.multiple_of(c * sw, sw), sw)
            product = jnp.dot(att[...], wo[:, part], preferred_element_type=F32)
            for half in range(halves):
                pb[c, :, :, half * rh : (half + 1) * rh] = (
                    product[half * sh : (half + 1) * sh]
                    .astype(BF16)
                    .reshape(lines, 2, rh, sw)
                )

            @pl.when(c < LINE_FIRST)
            def _():
                start_line(c, True)

            @pl.when(c >= LINE_FIRST)
            def _():
                y_copy(c).start()

        def start_line(c, wide):
            @pl.when(o == 0)
            def _():
                for line in range(lines - 1, 0, -1):
                    u_copy(c, line, wide).start()

            @pl.when(o == lines - 1)
            def _():
                for line in range(lines - 1):
                    d_copy(c, line, wide).start()

        loop(SCATTER_CHUNKS, partial)

        def paired(c):
            y_copy(c).wait_recv()
            pb[c, :, i] = (pb[c, :, i].astype(F32) + yb[c].astype(F32)).astype(BF16)
            start_line(c, False)

        def merge(c, line, wide, buffer):
            mine, theirs = rows_of(pb, c, line, wide), rows_of(buffer, c, line, wide)
            mine[...] = (mine[...].astype(F32) + theirs[...].astype(F32)).astype(BF16)

        def hop(c, wide):
            for line in range(lines - 1, 0, -1):

                @pl.when(line > o)
                def _():
                    u_copy(c, line, wide).wait_recv()
                    merge(c, line, wide, ub)
                    u_copy(c, line, wide).start()

        def hop_down(c, wide):
            for line in range(lines - 1):

                @pl.when(line < o)
                def _():
                    d_copy(c, line, wide).wait_recv()
                    merge(c, line, wide, db)
                    d_copy(c, line, wide).start()

        def ready(k):
            @pl.when(s < STEPS - 1)
            def _():
                for half in range(halves):
                    prepare(k + half * parts)

                @pl.when(k < GROUP)
                def _():
                    send_own(k)

                @pl.when(k == both % parts)
                def _():
                    h_copy(both, o, i, h_part, partner).start()

        def finish(c, wide):
            part = pl.ds(pl.multiple_of(c * sw, sw), sw)

            @pl.when(has_below)
            def _():
                u_copy(c, o, wide).wait_recv()
                merge(c, o, wide, ub)

            @pl.when(has_above)
            def _():
                d_copy(c, o, wide).wait_recv()
                merge(c, o, wide, db)

            if wide:
                y_copy_wide(c).start()
            else:
                out[:, part] += step_size * pb[c, o, i].astype(F32)

                @pl.when(
                    jnp.logical_and(c >= per_gather, c % per_gather == per_gather - 1)
                )
                def _():
                    ready(c // per_gather)

        def tick(at):
            @pl.when(jnp.logical_and(at >= LINE_FIRST, at < SCATTER_CHUNKS))
            def _():
                paired(at)

            for k in range(1, lines):
                c = at - k
                for wide, low, high in (
                    (True, 0, LINE_FIRST),
                    (False, LINE_FIRST, SCATTER_CHUNKS),
                ):
                    live = jnp.logical_and(c >= low, c < high)
                    if k < lines - 1:

                        @pl.when(jnp.logical_and(live, o == k))
                        def _():
                            hop(c, wide)

                        @pl.when(jnp.logical_and(live, lines - 1 - o == k))
                        def _():
                            hop_down(c, wide)
                    else:

                        @pl.when(live)
                        def _():
                            finish(c, wide)

        def finish_wide(c):
            part = pl.ds(pl.multiple_of(c * sw, sw), sw)
            y_copy_wide(c).wait_recv()
            out[:, part] += step_size * (pb[c, o, i].astype(F32) + yb[c, 0].astype(F32))

        def tick_all(at):
            tick(at)

            @pl.when(at == SCATTER_CHUNKS)
            def _():
                loop(LINE_FIRST, finish_wide)
                ready(0)

        loop(SCATTER_CHUNKS + lines - 1, tick_all)

        @pl.when(s < STEPS - 1)
        def _():
            prepare_scale()
            r_forward(o, True, True)

        def scatter_sends(c):
            for wide in (True, False):

                @pl.when((c < LINE_FIRST) == wide)
                def _():
                    (y_copy_wide if wide else y_copy)(c).wait_send()

                    def one(line):
                        @pl.when(jnp.logical_and(has_above, line > o))
                        def _():
                            u_copy(c, line, wide).wait_send()

                        @pl.when(jnp.logical_and(has_below, line < o))
                        def _():
                            d_copy(c, line, wide).wait_send()

                    loop(lines, one)

        loop(SCATTER_CHUNKS, scatter_sends)
        for h in range(heads):
            for half in range(halves):

                @pl.when(core == 0)
                def _():
                    kv_copy(s, t, h, half, kv_sib.at[h], sibling).wait_send()

                def chip_sends(other):
                    @pl.when(other > ch)
                    def _():
                        kv_copy(
                            s, t, h, half, kv_chip.at[h, other], other * 2 + core
                        ).wait_send()

                    @pl.when(other < ch)
                    def _():
                        kv_copy(
                            s, other * 2 + core, h, half, kv_fwd.at[h, other], sibling
                        ).wait_send()

                loop(chips, chip_sends)

    h_copy(both, o, i, h_part, partner).start()
    for c in range(GROUP):
        send_own(c)
    r_forward(o, True, True)
    loop(STEPS, step)


def shards(states, norm_gain, qkv_weight, qk_gain, out_weight, segment_lengths):
    tm_count, tp_count = lax.axis_size("tm"), lax.axis_size("tp")
    rows, width = states.shape
    head_cols = qkv_weight.shape[2]
    heads = head_cols // HD
    seg = rows * tp_count
    lines, chips = tp_count // 2, tm_count // 2
    halves = halves_of(rows)
    gw, sw = width * halves // GATHER_CHUNKS, width // SCATTER_CHUNKS
    dma = pltpu.SemaphoreType.DMA
    vmem = pl.BlockSpec(memory_space=pltpu.VMEM)
    smem = pl.BlockSpec(memory_space=pltpu.SMEM)
    hbm = pl.BlockSpec(memory_space=pl.ANY)
    g, s = GATHER_CHUNKS, SCATTER_CHUNKS
    return pl.pallas_call(
        functools.partial(kernel, tm_count, tp_count),
        out_shape=jax.ShapeDtypeStruct((rows, width), F32),
        in_specs=[vmem, vmem, hbm, vmem, hbm, smem],
        out_specs=vmem,
        scratch_shapes=[
            pltpu.VMEM((3, width, head_cols), BF16),
            pltpu.VMEM((head_cols, width), BF16),
            pltpu.VMEM((g, lines, 2, rows // halves, gw), BF16),
            pltpu.VMEM((lines, 2, 8, HD), F32),
            pltpu.VMEM((halves, 3, seg // halves, head_cols), F32),
            pltpu.VMEM((heads, seg, HD), BF16),
            pltpu.VMEM((STEPS, tm_count, heads, halves, 2, seg // halves, HD), BF16),
            pltpu.VMEM((seg, head_cols), BF16),
            pltpu.VMEM((heads, seg, HD), F32),
            pltpu.VMEM((heads, seg, 2 * HD), F32),
            pltpu.VMEM((s, lines, 2, rows, sw), BF16),
            pltpu.VMEM((s, lines, rows, sw), BF16),
            pltpu.VMEM((s, lines, 2, rows, sw), BF16),
            pltpu.VMEM((s, lines, 2, rows, sw), BF16),
            dma((width // gw,)),
            dma,
            dma((g, lines, 2)),
            dma((g, lines, 2)),
            dma((g, lines, 2)),
            dma((g, lines, 2)),
            dma((lines, 2)),
            dma((lines,)),
            dma((lines,)),
            dma((lines,)),
            dma((STEPS, tm_count, heads, halves)),
            dma((heads, halves)),
            dma((heads, chips, halves)),
            dma((heads, chips, halves)),
            dma((s,)),
            dma((s,)),
            dma((s, lines)),
            dma((s, lines)),
            dma((s, lines)),
            dma((s, lines)),
        ],
        compiler_params=pltpu.CompilerParams(
            collective_id=0, has_side_effects=True, vmem_limit_bytes=56 * 1024 * 1024
        ),
        cost_estimate=pl.CostEstimate(
            flops=STEPS * 2 * seg * width * head_cols * 4,
            bytes_accessed=width * head_cols * 8,
            transcendentals=STEPS * heads * seg * seg * tm_count,
        ),
    )(
        states,
        norm_gain.reshape(1, width),
        jnp.transpose(qkv_weight, (1, 0, 2)),
        qk_gain,
        out_weight,
        segment_lengths,
    )


def solution(mesh):
    return jax.shard_map(
        shards,
        mesh=mesh,
        in_specs=(
            P(("tm", "tp"), None),
            P(),
            P(None, None, "tp"),
            P(None, "tp"),
            P("tp", None),
            P(),
        ),
        out_specs=P(("tm", "tp"), None),
        check_vma=False,
    )
```

```python
import functools
import math

import jax
import jax.numpy as jnp
from jax import lax
from jax.experimental import pallas as pl
from jax.experimental.pallas import tpu as pltpu
from jax.sharding import PartitionSpec as P

HD = 128
STEPS = 2
GATHER_CHUNKS = 6
GROUP = 3
SCATTER_CHUNKS = 12
LINE_FIRST = 2

eps_norm = 1e-06
step_size = -0.5
BF16 = jnp.bfloat16
F32 = jnp.float32


def remote(src, dst, send_sem, recv_sem, tm, tp):
    return pltpu.make_async_remote_copy(
        src_ref=src,
        dst_ref=dst,
        send_sem=send_sem,
        recv_sem=recv_sem,
        device_id={"tm": tm, "tp": tp},
        device_id_type=pl.DeviceIdType.MESH,
    )


def halves_of(rows):
    return 2 if rows % 32 == 0 else 1


def loop(count, body):
    def step(index, carry):
        body(index)
        return carry

    lax.fori_loop(0, count, step, 0)


def kernel(
    tm_count, tp_count,
    states, gain, w_hbm, qk_gain, wo_hbm, lengths,
    out,
    w, wo, hb, rb, acc, qb, kv, att, run_max, run_acc, pb, yb, ub, db,
    w_sem, wo_sem,
    h_recv, h_part, h_up, h_down,
    r_recv, r_part, r_up, r_down,
    kv_recv, kv_sib, kv_chip, kv_fwd,
    y_send, y_recv, u_send, u_recv, d_send, d_recv,
):
    t, p = lax.axis_index("tm"), lax.axis_index("tp")
    lines, chips = tp_count // 2, tm_count // 2
    o, i = p // 2, p % 2
    ch, core = t // 2, t % 2
    partner, above, below = o * 2 + 1 - i, p + 2, p - 2
    sibling = ch * 2 + 1 - core
    has_above, has_below = o < lines - 1, o > 0
    rows, width = states.shape
    seg = rows * tp_count
    head_cols = w.shape[2]
    heads = head_cols // HD
    halves = halves_of(rows)
    rh, sh = rows // halves, seg // halves
    gw = width * halves // GATHER_CHUNKS
    sw = width // SCATTER_CHUNKS
    parts = width // gw
    per_gather = gw // sw
    both = GROUP

    def weight_copy(c):
        part = pl.ds(pl.multiple_of(c * gw, gw), gw)
        return pltpu.make_async_copy(w_hbm.at[:, part], w.at[:, part], w_sem.at[c])

    wo_copy = pltpu.make_async_copy(wo_hbm, wo, wo_sem)
    loop(parts, lambda c: weight_copy(c).start())
    wo_copy.start()

    barrier = pltpu.get_barrier_semaphore()

    def greet(tm, tp):
        pl.semaphore_signal(
            barrier, inc=1, device_id={"tm": tm, "tp": tp}, device_id_type=pl.DeviceIdType.MESH
        )

    greet(t, partner)
    greet(sibling, p)

    @pl.when(has_above)
    def _():
        greet(t, above)

    @pl.when(has_below)
    def _():
        greet(t, below)

    for other in range(chips):

        @pl.when(other != ch)
        def _():
            greet(other * 2 + core, p)

    out[...] = states[...]

    def prepare(c):
        part = pl.ds(pl.multiple_of(c % parts * gw, gw), gw)
        here = pl.ds(pl.multiple_of(c // parts * rh, rh), rh)
        hb[c, o, i] = (out[here, part] * gain[:, part]).astype(BF16)

    on_diagonal = lax.broadcasted_iota(
        jnp.int32, (rows, HD), 0
    ) == lax.broadcasted_iota(jnp.int32, (rows, HD), 1)

    def prepare_scale():
        square = jnp.zeros((rows, 1), F32)
        for c in range(SCATTER_CHUNKS):
            x = out[:, c * sw : (c + 1) * sw]
            square = square + jnp.sum(x * x, axis=-1, keepdims=True)
        scale = lax.rsqrt(square / width + eps_norm)
        laid = jnp.sum(jnp.where(on_diagonal, scale, 0.0), axis=0, keepdims=True)
        rb[o, i] = jnp.broadcast_to(laid, (8, HD))

    def scale_column(line, side):
        laid = jnp.broadcast_to(rb[line, side][0:1], (rows, HD))
        return jnp.sum(jnp.where(on_diagonal, laid, 0.0), axis=-1, keepdims=True)

    loop(GATHER_CHUNKS, prepare)
    prepare_scale()

    pl.semaphore_wait(
        barrier, 1 + chips + jnp.where(has_above, 1, 0) + jnp.where(has_below, 1, 0)
    )


    def h_copy(c, line, side, send_sem, tp):
        ref = hb.at[c, line, side]
        return remote(ref, ref, send_sem.at[c, line, side], h_recv.at[c, line, side], t, tp)

    def h_wait(c, line, side):
        h_copy(c, line, side, h_part, partner).wait_recv()

    def h_both_ways(c, line, side, up, down):
        if up:

            @pl.when(has_above)
            def _():
                h_copy(c, line, side, h_up, above).start()

        if down:

            @pl.when(has_below)
            def _():
                h_copy(c, line, side, h_down, below).start()

    def r_copy(line, side, send_sem, tp):
        ref = rb.at[line, side]
        return remote(ref, ref, send_sem.at[line], r_recv.at[line, side], t, tp)

    def r_forward(line, up, down):
        if up:

            @pl.when(has_above)
            def _():
                r_copy(line, i, r_up, above).start()

        if down:

            @pl.when(has_below)
            def _():
                r_copy(line, i, r_down, below).start()

        r_copy(line, i, r_part, partner).start()

    def send_own(c):
        h_both_ways(c, o, i, True, True)
        h_copy(c, o, i, h_part, partner).start()

    def kv_copy(s, seg_at, h, half, send_sem, tm):
        ref = kv.at[s, seg_at, h, half]
        return remote(ref, ref, send_sem.at[half], kv_recv.at[s, seg_at, h, half], tm, p)

    key_at = lax.broadcasted_iota(jnp.int32, (1, seg), 1)
    key_at = key_at % sh // rh * rows + key_at // sh * rh + key_at % rh
    ones = jnp.ones((seg, HD), BF16)

    def flash(s, h, segments, first):
        scores = [
            lax.dot_general(
                qb[h], kv[s, g, h, :, 0].reshape(seg, HD), (((1,), (1,)), ((), ())), preferred_element_type=F32
            )
            + jnp.where(key_at < lengths[g], 0.0, -1e30)
            for g in segments
        ]
        top = functools.reduce(jnp.maximum, scores)
        top = jnp.max(top, axis=-1, keepdims=True)
        if not first:
            old_top = run_max[h][:, :1]
            top = jnp.maximum(old_top, top)
        update = sum(
            jnp.dot(
                jnp.exp2(part - top).astype(BF16),
                jnp.concatenate([kv[s, g, h, :, 1].reshape(seg, HD), ones], axis=1),
                preferred_element_type=F32,
            )
            for part, g in zip(scores, segments)
        )
        if not first:
            update = update + run_acc[h] * jnp.exp2(old_top - top)
        run_max[h] = jnp.broadcast_to(top, (seg, HD))
        run_acc[h] = update

    def y_copy(c):
        return remote(
            pb.at[c, :, 1 - i], yb.at[c], y_send.at[c], y_recv.at[c], t, partner
        )

    def y_copy_wide(c):
        return remote(
            pb.at[c, o, 1 - i], yb.at[c, 0], y_send.at[c], y_recv.at[c], t, partner
        )

    def rows_of(buffer, c, line, wide):
        return buffer.at[c, line] if wide else buffer.at[c, line, i]

    def u_copy(c, line, wide):
        return remote(
            rows_of(pb, c, line, wide), rows_of(ub, c, line, wide),
            u_send.at[c, line], u_recv.at[c, line], t, above,
        )

    def d_copy(c, line, wide):
        return remote(
            rows_of(pb, c, line, wide), rows_of(db, c, line, wide),
            d_send.at[c, line], d_recv.at[c, line], t, below,
        )

    def step(s):
        def forward(c, distance):
            @pl.when(o >= distance)
            def _():
                line = o - distance
                h_wait(c, line, i)
                h_both_ways(c, line, i, True, False)
                h_copy(c, line, i, h_part, partner).start()

            @pl.when(o + distance < lines)
            def _():
                line = o + distance
                h_wait(c, line, i)
                h_both_ways(c, line, i, False, True)
                h_copy(c, line, i, h_part, partner).start()

        def forward_both(distance):
            for side in (i, 1 - i):

                @pl.when(o >= distance)
                def _():
                    h_wait(both, o - distance, side)
                    h_both_ways(both, o - distance, side, True, False)

                @pl.when(o + distance < lines)
                def _():
                    h_wait(both, o + distance, side)
                    h_both_ways(both, o + distance, side, False, True)

        def forward_scale(distance):
            @pl.when(o >= distance)
            def _():
                r_copy(o - distance, i, r_part, partner).wait_recv()
                r_forward(o - distance, True, False)

            @pl.when(o + distance < lines)
            def _():
                r_copy(o + distance, i, r_part, partner).wait_recv()
                r_forward(o + distance, False, True)

        def project(c):
            @pl.when(c != both)
            def _():
                for line in range(lines):
                    h_wait(c, line, 1 - i)

            @pl.when(jnp.logical_and(s == 0, c < parts))
            def _():
                weight_copy(c).wait()

            part = pl.ds(pl.multiple_of(c % parts * gw, gw), gw)
            h = hb[c].reshape(sh, gw)
            for j in range(3):
                acc[c // parts, j] += jnp.dot(h, w[j, part, :], preferred_element_type=F32)

        def scales(half):
            return jnp.concatenate(
                [
                    scale_column(line, side)[half * rh : (half + 1) * rh]
                    for line in range(lines)
                    for side in range(2)
                ],
                axis=0,
            )

        def emit_keys(half):
            scale = scales(half)
            for h in range(heads):
                cols = slice(h * HD, (h + 1) * HD)
                k = acc[half, 1, :, cols] * scale
                k_scale = lax.rsqrt(jnp.mean(k * k, axis=-1, keepdims=True) + eps_norm)
                kv[s, t, h, half, 0] = (k * k_scale * qk_gain[1:2, cols]).astype(BF16)
                kv[s, t, h, half, 1] = (acc[half, 2, :, cols] * scale).astype(BF16)
                for other in range(chips):

                    @pl.when(other > ch)
                    def _():
                        kv_copy(
                            s, t, h, half, kv_chip.at[h, other], other * 2 + core
                        ).start()

                @pl.when(core == 0)
                def _():
                    kv_copy(s, t, h, half, kv_sib.at[h], sibling).start()

        def emit_queries(half):
            scale = scales(half)
            for h in range(heads):
                cols = slice(h * HD, (h + 1) * HD)
                q = acc[half, 0, :, cols] * scale
                q_scale = lax.rsqrt(jnp.mean(q * q, axis=-1, keepdims=True) + eps_norm)
                q_scale = q_scale * (HD ** (-0.5) * math.log2(math.e))
                qb[h, half * sh : (half + 1) * sh] = (
                    q * q_scale * qk_gain[0:1, cols]
                ).astype(BF16)

        rest = GATHER_CHUNKS - GROUP - 1
        acc[...] = jnp.zeros_like(acc)
        for distance in range(1, lines - 1):
            loop(GROUP, lambda c: forward(c, distance))
            forward_scale(distance)
        loop(rest, lambda c: h_both_ways(c + both + 1, o, i, True, True))
        h_both_ways(both, o, i, True, True)
        h_wait(both, o, 1 - i)
        h_both_ways(both, o, 1 - i, True, True)
        loop(GROUP, lambda c: forward(c, lines - 1))
        forward_scale(lines - 1)
        loop(rest, lambda c: h_copy(c + both + 1, o, i, h_part, partner).start())
        for line in range(lines):
            r_copy(line, 1 - i, r_part, partner).wait_recv()

        for distance in range(1, lines - 1):

            def second(c):
                forward(c + both + 1, distance)
                if distance == 1:
                    project(c)

            loop(rest, second)
            forward_both(distance)
            if distance == 1:
                loop(GROUP - rest, lambda c: project(c + rest))
                if halves == 2:
                    emit_keys(0)
            elif distance == 2 and halves == 2:
                emit_queries(0)

        loop(rest, lambda c: forward(c + both + 1, lines - 1))

        def final(c):
            @pl.when(c == rest)
            def _():
                forward_both(lines - 1)

            project(jnp.where(c == rest, both, c + both + 1))

        loop(rest + 1, final)
        emit_keys(halves - 1)
        emit_queries(halves - 1)

        def pass_on(pair, part):
            def one(other):
                @pl.when(other < ch)
                def _():
                    for h in pair:
                        for half in part:
                            got = kv_copy(
                                s, other * 2 + core, h, half, kv_fwd.at[h, other], sibling
                            )
                            got.wait_recv()
                            got.start()

            loop(chips, one)

        pass_on(range(heads), range(halves - 1))
        for h in range(heads):
            flash(s, h, [t], True)

        @pl.when(s == 0)
        def _():
            wo_copy.wait()

        def gather_sends(c):
            def one(line):
                h_copy(c, line, i, h_part, partner).wait_send()
                way_sends(c, line, i)

            loop(lines, one)

        def scale_sends(line):
            r_copy(line, i, r_part, partner).wait_send()

            @pl.when(jnp.logical_and(has_above, line <= o))
            def _():
                r_copy(line, i, r_up, above).wait_send()

            @pl.when(jnp.logical_and(has_below, line >= o))
            def _():
                r_copy(line, i, r_down, below).wait_send()

        def way_sends(c, line, side):
            @pl.when(jnp.logical_and(has_above, line <= o))
            def _():
                h_copy(c, line, side, h_up, above).wait_send()

            @pl.when(jnp.logical_and(has_below, line >= o))
            def _():
                h_copy(c, line, side, h_down, below).wait_send()

        def both_sends(line):
            way_sends(both, line, i)
            way_sends(both, line, 1 - i)

        def chunk_sends(c):
            @pl.when(c != both)
            def _():
                gather_sends(c)

        loop(GATHER_CHUNKS, chunk_sends)
        h_copy(both, o, i, h_part, partner).wait_send()
        loop(lines, both_sends)
        loop(lines, scale_sends)

        @pl.when(core == 1)
        def _():
            for h in range(heads):
                for half in range(halves):
                    kv_copy(s, t - 1, h, half, kv_sib.at[h], sibling).wait_recv()
            for h in range(heads):
                flash(s, h, [t - 1], False)

        pairs = [range(h, min(h + 2, heads)) for h in range(0, heads, 2)]
        for pair in pairs:
            pass_on(pair, range(halves - 1, halves))

            def direct(other):
                @pl.when(other < ch)
                def _():
                    for h in pair:
                        flash(s, h, [other * 2 + core], False)

            loop(chips, direct)
        for pair in pairs:

            def passed(other):
                @pl.when(other < ch)
                def _():
                    g = other * 2 + 1 - core
                    for h in pair:
                        for half in range(halves):
                            kv_copy(s, g, h, half, kv_fwd.at[h, other], sibling).wait_recv()
                    for h in pair:
                        flash(s, h, [g], False)

            loop(chips, passed)
        for h in range(heads):
            att[:, h * HD : (h + 1) * HD] = (
                run_acc[h][:, :HD] / run_acc[h][:, HD:]
            ).astype(BF16)

        def partial(c):
            part = pl.ds(pl.multiple_of(c * sw, sw), sw)
            product = jnp.dot(att[...], wo[:, part], preferred_element_type=F32)
            for half in range(halves):
                pb[c, :, :, half * rh : (half + 1) * rh] = (
                    product[half * sh : (half + 1) * sh]
                    .astype(BF16)
                    .reshape(lines, 2, rh, sw)
                )

            @pl.when(c < LINE_FIRST)
            def _():
                start_line(c, True)

            @pl.when(c >= LINE_FIRST)
            def _():
                y_copy(c).start()

        def start_line(c, wide):
            @pl.when(o == 0)
            def _():
                for line in range(lines - 1, 0, -1):
                    u_copy(c, line, wide).start()

            @pl.when(o == lines - 1)
            def _():
                for line in range(lines - 1):
                    d_copy(c, line, wide).start()

        loop(SCATTER_CHUNKS, partial)

        def paired(c):
            y_copy(c).wait_recv()
            pb[c, :, i] = (pb[c, :, i].astype(F32) + yb[c].astype(F32)).astype(BF16)
            start_line(c, False)

        def merge(c, line, wide, buffer):
            mine, theirs = rows_of(pb, c, line, wide), rows_of(buffer, c, line, wide)
            mine[...] = (mine[...].astype(F32) + theirs[...].astype(F32)).astype(BF16)

        def hop(c, wide):
            for line in range(lines - 1, 0, -1):

                @pl.when(line > o)
                def _():
                    u_copy(c, line, wide).wait_recv()
                    merge(c, line, wide, ub)
                    u_copy(c, line, wide).start()

        def hop_down(c, wide):
            for line in range(lines - 1):

                @pl.when(line < o)
                def _():
                    d_copy(c, line, wide).wait_recv()
                    merge(c, line, wide, db)
                    d_copy(c, line, wide).start()

        def ready(k):
            @pl.when(s < STEPS - 1)
            def _():
                for half in range(halves):
                    prepare(k + half * parts)

                @pl.when(k < GROUP)
                def _():
                    send_own(k)

                @pl.when(k == both % parts)
                def _():
                    h_copy(both, o, i, h_part, partner).start()

        def finish(c, wide):
            part = pl.ds(pl.multiple_of(c * sw, sw), sw)

            @pl.when(has_below)
            def _():
                u_copy(c, o, wide).wait_recv()
                merge(c, o, wide, ub)

            @pl.when(has_above)
            def _():
                d_copy(c, o, wide).wait_recv()
                merge(c, o, wide, db)

            if wide:
                y_copy_wide(c).start()
            else:
                out[:, part] += step_size * pb[c, o, i].astype(F32)

                @pl.when(
                    jnp.logical_and(c >= per_gather, c % per_gather == per_gather - 1)
                )
                def _():
                    ready(c // per_gather)

        def tick(at):
            @pl.when(jnp.logical_and(at >= LINE_FIRST, at < SCATTER_CHUNKS))
            def _():
                paired(at)

            for k in range(1, lines):
                c = at - k
                for wide, low, high in (
                    (True, 0, LINE_FIRST),
                    (False, LINE_FIRST, SCATTER_CHUNKS),
                ):
                    live = jnp.logical_and(c >= low, c < high)
                    if k < lines - 1:

                        @pl.when(jnp.logical_and(live, o == k))
                        def _():
                            hop(c, wide)

                        @pl.when(jnp.logical_and(live, lines - 1 - o == k))
                        def _():
                            hop_down(c, wide)
                    else:

                        @pl.when(live)
                        def _():
                            finish(c, wide)

        def finish_wide(c):
            part = pl.ds(pl.multiple_of(c * sw, sw), sw)
            y_copy_wide(c).wait_recv()
            out[:, part] += step_size * (pb[c, o, i].astype(F32) + yb[c, 0].astype(F32))

        def tick_all(at):
            tick(at)

            @pl.when(at == SCATTER_CHUNKS)
            def _():
                loop(LINE_FIRST, finish_wide)
                ready(0)

        loop(SCATTER_CHUNKS + lines - 1, tick_all)

        @pl.when(s < STEPS - 1)
        def _():
            prepare_scale()
            r_forward(o, True, True)

        def scatter_sends(c):
            for wide in (True, False):

                @pl.when((c < LINE_FIRST) == wide)
                def _():
                    (y_copy_wide if wide else y_copy)(c).wait_send()

                    def one(line):
                        @pl.when(jnp.logical_and(has_above, line > o))
                        def _():
                            u_copy(c, line, wide).wait_send()

                        @pl.when(jnp.logical_and(has_below, line < o))
                        def _():
                            d_copy(c, line, wide).wait_send()

                    loop(lines, one)

        loop(SCATTER_CHUNKS, scatter_sends)
        for h in range(heads):
            for half in range(halves):

                @pl.when(core == 0)
                def _():
                    kv_copy(s, t, h, half, kv_sib.at[h], sibling).wait_send()

                def chip_sends(other):
                    @pl.when(other > ch)
                    def _():
                        kv_copy(
                            s, t, h, half, kv_chip.at[h, other], other * 2 + core
                        ).wait_send()

                    @pl.when(other < ch)
                    def _():
                        kv_copy(
                            s, other * 2 + core, h, half, kv_fwd.at[h, other], sibling
                        ).wait_send()

                loop(chips, chip_sends)

    h_copy(both, o, i, h_part, partner).start()
    for c in range(GROUP):
        send_own(c)
    r_forward(o, True, True)
    loop(STEPS, step)


def shards(states, norm_gain, qkv_weight, qk_gain, out_weight, segment_lengths):
    tm_count, tp_count = lax.axis_size("tm"), lax.axis_size("tp")
    rows, width = states.shape
    head_cols = qkv_weight.shape[2]
    heads = head_cols // HD
    seg = rows * tp_count
    lines, chips = tp_count // 2, tm_count // 2
    halves = halves_of(rows)
    gw, sw = width * halves // GATHER_CHUNKS, width // SCATTER_CHUNKS
    dma = pltpu.SemaphoreType.DMA
    vmem = pl.BlockSpec(memory_space=pltpu.VMEM)
    smem = pl.BlockSpec(memory_space=pltpu.SMEM)
    hbm = pl.BlockSpec(memory_space=pl.ANY)
    g, s = GATHER_CHUNKS, SCATTER_CHUNKS
    return pl.pallas_call(
        functools.partial(kernel, tm_count, tp_count),
        out_shape=jax.ShapeDtypeStruct((rows, width), F32),
        in_specs=[vmem, vmem, hbm, vmem, hbm, smem],
        out_specs=vmem,
        scratch_shapes=[
            pltpu.VMEM((3, width, head_cols), BF16),
            pltpu.VMEM((head_cols, width), BF16),
            pltpu.VMEM((g, lines, 2, rows // halves, gw), BF16),
            pltpu.VMEM((lines, 2, 8, HD), F32),
            pltpu.VMEM((halves, 3, seg // halves, head_cols), F32),
            pltpu.VMEM((heads, seg, HD), BF16),
            pltpu.VMEM((STEPS, tm_count, heads, halves, 2, seg // halves, HD), BF16),
            pltpu.VMEM((seg, head_cols), BF16),
            pltpu.VMEM((heads, seg, HD), F32),
            pltpu.VMEM((heads, seg, 2 * HD), F32),
            pltpu.VMEM((s, lines, 2, rows, sw), BF16),
            pltpu.VMEM((s, lines, rows, sw), BF16),
            pltpu.VMEM((s, lines, 2, rows, sw), BF16),
            pltpu.VMEM((s, lines, 2, rows, sw), BF16),
            dma((width // gw,)),
            dma,
            dma((g, lines, 2)),
            dma((g, lines, 2)),
            dma((g, lines, 2)),
            dma((g, lines, 2)),
            dma((lines, 2)),
            dma((lines,)),
            dma((lines,)),
            dma((lines,)),
            dma((STEPS, tm_count, heads, halves)),
            dma((heads, halves)),
            dma((heads, chips, halves)),
            dma((heads, chips, halves)),
            dma((s,)),
            dma((s,)),
            dma((s, lines)),
            dma((s, lines)),
            dma((s, lines)),
            dma((s, lines)),
        ],
        compiler_params=pltpu.CompilerParams(
            collective_id=0, has_side_effects=True, vmem_limit_bytes=56 * 1024 * 1024
        ),
        cost_estimate=pl.CostEstimate(
            flops=STEPS * 2 * seg * width * head_cols * 4,
            bytes_accessed=width * head_cols * 8,
            transcendentals=STEPS * heads * seg * seg * tm_count,
        ),
    )(
        states,
        norm_gain.reshape(1, width),
        jnp.transpose(qkv_weight, (1, 0, 2)),
        qk_gain,
        out_weight,
        segment_lengths,
    )


def solution(mesh):
    return jax.shard_map(
        shards,
        mesh=mesh,
        in_specs=(
            P(("tm", "tp"), None),
            P(),
            P(None, None, "tp"),
            P(None, "tp"),
            P("tp", None),
            P(),
        ),
        out_specs=P(("tm", "tp"), None),
        check_vma=False,
    )
```

```python
import functools
import math

import jax
import jax.numpy as jnp
from jax import lax
from jax.experimental import pallas as pl
from jax.experimental.pallas import tpu as pltpu
from jax.sharding import PartitionSpec as P

HD = 128
STEPS = 2
GATHER_CHUNKS = 6
GROUP = 3
SCATTER_CHUNKS = 24
LINE_FIRST = 4

eps_norm = 1e-06
step_size = -0.5
BF16 = jnp.bfloat16
F32 = jnp.float32


def remote(src, dst, send_sem, recv_sem, tm, tp):
    return pltpu.make_async_remote_copy(
        src_ref=src,
        dst_ref=dst,
        send_sem=send_sem,
        recv_sem=recv_sem,
        device_id={"tm": tm, "tp": tp},
        device_id_type=pl.DeviceIdType.MESH,
    )


def halves_of(rows):
    return 2 if rows % 32 == 0 else 1


def loop(count, body):
    def step(index, carry):
        body(index)
        return carry

    lax.fori_loop(0, count, step, 0)


def kernel(
    tm_count, tp_count,
    states, gain, w_hbm, qk_gain, wo_hbm, lengths,
    out,
    w, wo, hb, rb, acc, qb, kv, att, run_max, run_acc, pb, yb, ub, db,
    w_sem, wo_sem,
    h_recv, h_part, h_up, h_down,
    r_recv, r_part, r_up, r_down,
    kv_recv, kv_sib, kv_chip, kv_fwd,
    y_send, y_recv, u_send, u_recv, d_send, d_recv,
):
    t, p = lax.axis_index("tm"), lax.axis_index("tp")
    lines, chips = tp_count // 2, tm_count // 2
    o, i = p // 2, p % 2
    ch, core = t // 2, t % 2
    partner, above, below = o * 2 + 1 - i, p + 2, p - 2
    sibling = ch * 2 + 1 - core
    has_above, has_below = o < lines - 1, o > 0
    rows, width = states.shape
    seg = rows * tp_count
    head_cols = w.shape[2]
    heads = head_cols // HD
    halves = halves_of(rows)
    rh, sh = rows // halves, seg // halves
    gw = width * halves // GATHER_CHUNKS
    sw = width // SCATTER_CHUNKS
    parts = width // gw
    per_gather = gw // sw
    both = GROUP

    def weight_copy(c):
        part = pl.ds(pl.multiple_of(c * gw, gw), gw)
        return pltpu.make_async_copy(w_hbm.at[:, part], w.at[:, part], w_sem.at[c])

    wo_copy = pltpu.make_async_copy(wo_hbm, wo, wo_sem)
    loop(parts, lambda c: weight_copy(c).start())
    wo_copy.start()

    barrier = pltpu.get_barrier_semaphore()

    def greet(tm, tp):
        pl.semaphore_signal(
            barrier, inc=1, device_id={"tm": tm, "tp": tp}, device_id_type=pl.DeviceIdType.MESH
        )

    greet(t, partner)
    greet(sibling, p)

    @pl.when(has_above)
    def _():
        greet(t, above)

    @pl.when(has_below)
    def _():
        greet(t, below)

    for other in range(chips):

        @pl.when(other != ch)
        def _():
            greet(other * 2 + core, p)

    out[...] = states[...]

    def prepare(c):
        part = pl.ds(pl.multiple_of(c % parts * gw, gw), gw)
        here = pl.ds(pl.multiple_of(c // parts * rh, rh), rh)
        hb[c, o, i] = (out[here, part] * gain[:, part]).astype(BF16)

    on_diagonal = lax.broadcasted_iota(
        jnp.int32, (rows, HD), 0
    ) == lax.broadcasted_iota(jnp.int32, (rows, HD), 1)

    def prepare_scale():
        square = jnp.zeros((rows, 1), F32)
        for c in range(SCATTER_CHUNKS):
            x = out[:, c * sw : (c + 1) * sw]
            square = square + jnp.sum(x * x, axis=-1, keepdims=True)
        scale = lax.rsqrt(square / width + eps_norm)
        laid = jnp.sum(jnp.where(on_diagonal, scale, 0.0), axis=0, keepdims=True)
        rb[o, i] = jnp.broadcast_to(laid, (8, HD))

    def scale_column(line, side):
        laid = jnp.broadcast_to(rb[line, side][0:1], (rows, HD))
        return jnp.sum(jnp.where(on_diagonal, laid, 0.0), axis=-1, keepdims=True)

    loop(GATHER_CHUNKS, prepare)
    prepare_scale()

    pl.semaphore_wait(
        barrier, 1 + chips + jnp.where(has_above, 1, 0) + jnp.where(has_below, 1, 0)
    )


    def h_copy(c, line, side, send_sem, tp):
        ref = hb.at[c, line, side]
        return remote(ref, ref, send_sem.at[c, line, side], h_recv.at[c, line, side], t, tp)

    def h_wait(c, line, side):
        h_copy(c, line, side, h_part, partner).wait_recv()

    def h_both_ways(c, line, side, up, down):
        if up:

            @pl.when(has_above)
            def _():
                h_copy(c, line, side, h_up, above).start()

        if down:

            @pl.when(has_below)
            def _():
                h_copy(c, line, side, h_down, below).start()

    def r_copy(line, side, send_sem, tp):
        ref = rb.at[line, side]
        return remote(ref, ref, send_sem.at[line], r_recv.at[line, side], t, tp)

    def r_forward(line, up, down):
        if up:

            @pl.when(has_above)
            def _():
                r_copy(line, i, r_up, above).start()

        if down:

            @pl.when(has_below)
            def _():
                r_copy(line, i, r_down, below).start()

        r_copy(line, i, r_part, partner).start()

    def send_own(c):
        h_both_ways(c, o, i, True, True)
        h_copy(c, o, i, h_part, partner).start()

    def kv_copy(s, seg_at, h, half, send_sem, tm):
        ref = kv.at[s, seg_at, h, half]
        return remote(ref, ref, send_sem.at[half], kv_recv.at[s, seg_at, h, half], tm, p)

    key_at = lax.broadcasted_iota(jnp.int32, (1, seg), 1)
    key_at = key_at % sh // rh * rows + key_at // sh * rh + key_at % rh
    ones = jnp.ones((seg, HD), BF16)

    def flash(s, h, segments, first):
        scores = [
            lax.dot_general(
                qb[h], kv[s, g, h, :, 0].reshape(seg, HD), (((1,), (1,)), ((), ())), preferred_element_type=F32
            )
            + jnp.where(key_at < lengths[g], 0.0, -1e30)
            for g in segments
        ]
        top = functools.reduce(jnp.maximum, scores)
        top = jnp.max(top, axis=-1, keepdims=True)
        if not first:
            old_top = run_max[h][:, :1]
            top = jnp.maximum(old_top, top)
        update = sum(
            jnp.dot(
                jnp.exp2(part - top).astype(BF16),
                jnp.concatenate([kv[s, g, h, :, 1].reshape(seg, HD), ones], axis=1),
                preferred_element_type=F32,
            )
            for part, g in zip(scores, segments)
        )
        if not first:
            update = update + run_acc[h] * jnp.exp2(old_top - top)
        run_max[h] = jnp.broadcast_to(top, (seg, HD))
        run_acc[h] = update

    def y_copy(c):
        return remote(
            pb.at[c, :, 1 - i], yb.at[c], y_send.at[c], y_recv.at[c], t, partner
        )

    def y_copy_wide(c):
        return remote(
            pb.at[c, o, 1 - i], yb.at[c, 0], y_send.at[c], y_recv.at[c], t, partner
        )

    def rows_of(buffer, c, line, wide):
        return buffer.at[c, line] if wide else buffer.at[c, line, i]

    def u_copy(c, line, wide):
        return remote(
            rows_of(pb, c, line, wide), rows_of(ub, c, line, wide),
            u_send.at[c, line], u_recv.at[c, line], t, above,
        )

    def d_copy(c, line, wide):
        return remote(
            rows_of(pb, c, line, wide), rows_of(db, c, line, wide),
            d_send.at[c, line], d_recv.at[c, line], t, below,
        )

    def step(s):
        def forward(c, distance):
            @pl.when(o >= distance)
            def _():
                line = o - distance
                h_wait(c, line, i)
                h_both_ways(c, line, i, True, False)
                h_copy(c, line, i, h_part, partner).start()

            @pl.when(o + distance < lines)
            def _():
                line = o + distance
                h_wait(c, line, i)
                h_both_ways(c, line, i, False, True)
                h_copy(c, line, i, h_part, partner).start()

        def forward_both(distance):
            for side in (i, 1 - i):

                @pl.when(o >= distance)
                def _():
                    h_wait(both, o - distance, side)
                    h_both_ways(both, o - distance, side, True, False)

                @pl.when(o + distance < lines)
                def _():
                    h_wait(both, o + distance, side)
                    h_both_ways(both, o + distance, side, False, True)

        def forward_scale(distance):
            @pl.when(o >= distance)
            def _():
                r_copy(o - distance, i, r_part, partner).wait_recv()
                r_forward(o - distance, True, False)

            @pl.when(o + distance < lines)
            def _():
                r_copy(o + distance, i, r_part, partner).wait_recv()
                r_forward(o + distance, False, True)

        def project(c):
            @pl.when(c != both)
            def _():
                for line in range(lines):
                    h_wait(c, line, 1 - i)

            @pl.when(jnp.logical_and(s == 0, c < parts))
            def _():
                weight_copy(c).wait()

            part = pl.ds(pl.multiple_of(c % parts * gw, gw), gw)
            h = hb[c].reshape(sh, gw)
            for j in range(3):
                acc[c // parts, j] += jnp.dot(h, w[j, part, :], preferred_element_type=F32)

        def scales(half):
            return jnp.concatenate(
                [
                    scale_column(line, side)[half * rh : (half + 1) * rh]
                    for line in range(lines)
                    for side in range(2)
                ],
                axis=0,
            )

        def emit_keys(half):
            scale = scales(half)
            for h in range(heads):
                cols = slice(h * HD, (h + 1) * HD)
                k = acc[half, 1, :, cols] * scale
                k_scale = lax.rsqrt(jnp.mean(k * k, axis=-1, keepdims=True) + eps_norm)
                kv[s, t, h, half, 0] = (k * k_scale * qk_gain[1:2, cols]).astype(BF16)
                kv[s, t, h, half, 1] = (acc[half, 2, :, cols] * scale).astype(BF16)
                for other in range(chips):

                    @pl.when(other > ch)
                    def _():
                        kv_copy(
                            s, t, h, half, kv_chip.at[h, other], other * 2 + core
                        ).start()

                @pl.when(core == 0)
                def _():
                    kv_copy(s, t, h, half, kv_sib.at[h], sibling).start()

        def emit_queries(half):
            scale = scales(half)
            for h in range(heads):
                cols = slice(h * HD, (h + 1) * HD)
                q = acc[half, 0, :, cols] * scale
                q_scale = lax.rsqrt(jnp.mean(q * q, axis=-1, keepdims=True) + eps_norm)
                q_scale = q_scale * (HD ** (-0.5) * math.log2(math.e))
                qb[h, half * sh : (half + 1) * sh] = (
                    q * q_scale * qk_gain[0:1, cols]
                ).astype(BF16)

        rest = GATHER_CHUNKS - GROUP - 1
        acc[...] = jnp.zeros_like(acc)
        for distance in range(1, lines - 1):
            loop(GROUP, lambda c: forward(c, distance))
            forward_scale(distance)
        loop(rest, lambda c: h_both_ways(c + both + 1, o, i, True, True))
        h_both_ways(both, o, i, True, True)
        h_wait(both, o, 1 - i)
        h_both_ways(both, o, 1 - i, True, True)
        loop(GROUP, lambda c: forward(c, lines - 1))
        forward_scale(lines - 1)
        loop(rest, lambda c: h_copy(c + both + 1, o, i, h_part, partner).start())
        for line in range(lines):
            r_copy(line, 1 - i, r_part, partner).wait_recv()

        for distance in range(1, lines - 1):

            def second(c):
                forward(c + both + 1, distance)
                if distance == 1:
                    project(c)

            loop(rest, second)
            forward_both(distance)
            if distance == 1:
                loop(GROUP - rest, lambda c: project(c + rest))
                if halves == 2:
                    emit_keys(0)
            elif distance == 2 and halves == 2:
                emit_queries(0)

        loop(rest, lambda c: forward(c + both + 1, lines - 1))

        def final(c):
            @pl.when(c == rest)
            def _():
                forward_both(lines - 1)

            project(jnp.where(c == rest, both, c + both + 1))

        loop(rest + 1, final)
        emit_keys(halves - 1)
        emit_queries(halves - 1)

        def pass_on(pair, part):
            def one(other):
                @pl.when(other < ch)
                def _():
                    for h in pair:
                        for half in part:
                            got = kv_copy(
                                s, other * 2 + core, h, half, kv_fwd.at[h, other], sibling
                            )
                            got.wait_recv()
                            got.start()

            loop(chips, one)

        pass_on(range(heads), range(halves - 1))
        for h in range(heads):
            flash(s, h, [t], True)

        @pl.when(s == 0)
        def _():
            wo_copy.wait()

        def gather_sends(c):
            def one(line):
                h_copy(c, line, i, h_part, partner).wait_send()
                way_sends(c, line, i)

            loop(lines, one)

        def scale_sends(line):
            r_copy(line, i, r_part, partner).wait_send()

            @pl.when(jnp.logical_and(has_above, line <= o))
            def _():
                r_copy(line, i, r_up, above).wait_send()

            @pl.when(jnp.logical_and(has_below, line >= o))
            def _():
                r_copy(line, i, r_down, below).wait_send()

        def way_sends(c, line, side):
            @pl.when(jnp.logical_and(has_above, line <= o))
            def _():
                h_copy(c, line, side, h_up, above).wait_send()

            @pl.when(jnp.logical_and(has_below, line >= o))
            def _():
                h_copy(c, line, side, h_down, below).wait_send()

        def both_sends(line):
            way_sends(both, line, i)
            way_sends(both, line, 1 - i)

        def chunk_sends(c):
            @pl.when(c != both)
            def _():
                gather_sends(c)

        loop(GATHER_CHUNKS, chunk_sends)
        h_copy(both, o, i, h_part, partner).wait_send()
        loop(lines, both_sends)
        loop(lines, scale_sends)

        @pl.when(core == 1)
        def _():
            for h in range(heads):
                for half in range(halves):
                    kv_copy(s, t - 1, h, half, kv_sib.at[h], sibling).wait_recv()
            for h in range(heads):
                flash(s, h, [t - 1], False)

        pairs = [range(h, min(h + 2, heads)) for h in range(0, heads, 2)]
        for pair in pairs:
            pass_on(pair, range(halves - 1, halves))

            def direct(other):
                @pl.when(other < ch)
                def _():
                    for h in pair:
                        flash(s, h, [other * 2 + core], False)

            loop(chips, direct)
        for pair in pairs:

            def passed(other):
                @pl.when(other < ch)
                def _():
                    g = other * 2 + 1 - core
                    for h in pair:
                        for half in range(halves):
                            kv_copy(s, g, h, half, kv_fwd.at[h, other], sibling).wait_recv()
                    for h in pair:
                        flash(s, h, [g], False)

            loop(chips, passed)
        for h in range(heads):
            att[:, h * HD : (h + 1) * HD] = (
                run_acc[h][:, :HD] / run_acc[h][:, HD:]
            ).astype(BF16)

        def partial(c):
            part = pl.ds(pl.multiple_of(c * sw, sw), sw)
            product = jnp.dot(att[...], wo[:, part], preferred_element_type=F32)
            for half in range(halves):
                pb[c, :, :, half * rh : (half + 1) * rh] = (
                    product[half * sh : (half + 1) * sh]
                    .astype(BF16)
                    .reshape(lines, 2, rh, sw)
                )

            @pl.when(c < LINE_FIRST)
            def _():
                start_line(c, True)

            @pl.when(c >= LINE_FIRST)
            def _():
                y_copy(c).start()

        def start_line(c, wide):
            @pl.when(o == 0)
            def _():
                for line in range(lines - 1, 0, -1):
                    u_copy(c, line, wide).start()

            @pl.when(o == lines - 1)
            def _():
                for line in range(lines - 1):
                    d_copy(c, line, wide).start()

        loop(SCATTER_CHUNKS, partial)

        def paired(c):
            y_copy(c).wait_recv()
            pb[c, :, i] = (pb[c, :, i].astype(F32) + yb[c].astype(F32)).astype(BF16)
            start_line(c, False)

        def merge(c, line, wide, buffer):
            mine, theirs = rows_of(pb, c, line, wide), rows_of(buffer, c, line, wide)
            mine[...] = (mine[...].astype(F32) + theirs[...].astype(F32)).astype(BF16)

        def hop(c, wide):
            for line in range(lines - 1, 0, -1):

                @pl.when(line > o)
                def _():
                    u_copy(c, line, wide).wait_recv()
                    merge(c, line, wide, ub)
                    u_copy(c, line, wide).start()

        def hop_down(c, wide):
            for line in range(lines - 1):

                @pl.when(line < o)
                def _():
                    d_copy(c, line, wide).wait_recv()
                    merge(c, line, wide, db)
                    d_copy(c, line, wide).start()

        def ready(k):
            @pl.when(s < STEPS - 1)
            def _():
                for half in range(halves):
                    prepare(k + half * parts)

                @pl.when(k < GROUP)
                def _():
                    send_own(k)

                @pl.when(k == both % parts)
                def _():
                    h_copy(both, o, i, h_part, partner).start()

        def finish(c, wide):
            part = pl.ds(pl.multiple_of(c * sw, sw), sw)

            @pl.when(has_below)
            def _():
                u_copy(c, o, wide).wait_recv()
                merge(c, o, wide, ub)

            @pl.when(has_above)
            def _():
                d_copy(c, o, wide).wait_recv()
                merge(c, o, wide, db)

            if wide:
                y_copy_wide(c).start()
            else:
                out[:, part] += step_size * pb[c, o, i].astype(F32)

                @pl.when(
                    jnp.logical_and(c >= per_gather, c % per_gather == per_gather - 1)
                )
                def _():
                    ready(c // per_gather)

        def tick(at):
            @pl.when(jnp.logical_and(at >= LINE_FIRST, at < SCATTER_CHUNKS))
            def _():
                paired(at)

            for k in range(1, lines):
                c = at - k
                for wide, low, high in (
                    (True, 0, LINE_FIRST),
                    (False, LINE_FIRST, SCATTER_CHUNKS),
                ):
                    live = jnp.logical_and(c >= low, c < high)
                    if k < lines - 1:

                        @pl.when(jnp.logical_and(live, o == k))
                        def _():
                            hop(c, wide)

                        @pl.when(jnp.logical_and(live, lines - 1 - o == k))
                        def _():
                            hop_down(c, wide)
                    else:

                        @pl.when(live)
                        def _():
                            finish(c, wide)

        def finish_wide(c):
            part = pl.ds(pl.multiple_of(c * sw, sw), sw)
            y_copy_wide(c).wait_recv()
            out[:, part] += step_size * (pb[c, o, i].astype(F32) + yb[c, 0].astype(F32))

        def tick_all(at):
            tick(at)

            @pl.when(at == SCATTER_CHUNKS)
            def _():
                loop(LINE_FIRST, finish_wide)
                ready(0)

        loop(SCATTER_CHUNKS + lines - 1, tick_all)

        @pl.when(s < STEPS - 1)
        def _():
            prepare_scale()
            r_forward(o, True, True)

        def scatter_sends(c):
            for wide in (True, False):

                @pl.when((c < LINE_FIRST) == wide)
                def _():
                    (y_copy_wide if wide else y_copy)(c).wait_send()

                    def one(line):
                        @pl.when(jnp.logical_and(has_above, line > o))
                        def _():
                            u_copy(c, line, wide).wait_send()

                        @pl.when(jnp.logical_and(has_below, line < o))
                        def _():
                            d_copy(c, line, wide).wait_send()

                    loop(lines, one)

        loop(SCATTER_CHUNKS, scatter_sends)
        for h in range(heads):
            for half in range(halves):

                @pl.when(core == 0)
                def _():
                    kv_copy(s, t, h, half, kv_sib.at[h], sibling).wait_send()

                def chip_sends(other):
                    @pl.when(other > ch)
                    def _():
                        kv_copy(
                            s, t, h, half, kv_chip.at[h, other], other * 2 + core
                        ).wait_send()

                    @pl.when(other < ch)
                    def _():
                        kv_copy(
                            s, other * 2 + core, h, half, kv_fwd.at[h, other], sibling
                        ).wait_send()

                loop(chips, chip_sends)

    h_copy(both, o, i, h_part, partner).start()
    for c in range(GROUP):
        send_own(c)
    r_forward(o, True, True)
    loop(STEPS, step)


def shards(states, norm_gain, qkv_weight, qk_gain, out_weight, segment_lengths):
    tm_count, tp_count = lax.axis_size("tm"), lax.axis_size("tp")
    rows, width = states.shape
    head_cols = qkv_weight.shape[2]
    heads = head_cols // HD
    seg = rows * tp_count
    lines, chips = tp_count // 2, tm_count // 2
    halves = halves_of(rows)
    gw, sw = width * halves // GATHER_CHUNKS, width // SCATTER_CHUNKS
    dma = pltpu.SemaphoreType.DMA
    vmem = pl.BlockSpec(memory_space=pltpu.VMEM)
    smem = pl.BlockSpec(memory_space=pltpu.SMEM)
    hbm = pl.BlockSpec(memory_space=pl.ANY)
    g, s = GATHER_CHUNKS, SCATTER_CHUNKS
    return pl.pallas_call(
        functools.partial(kernel, tm_count, tp_count),
        out_shape=jax.ShapeDtypeStruct((rows, width), F32),
        in_specs=[vmem, vmem, hbm, vmem, hbm, smem],
        out_specs=vmem,
        scratch_shapes=[
            pltpu.VMEM((3, width, head_cols), BF16),
            pltpu.VMEM((head_cols, width), BF16),
            pltpu.VMEM((g, lines, 2, rows // halves, gw), BF16),
            pltpu.VMEM((lines, 2, 8, HD), F32),
            pltpu.VMEM((halves, 3, seg // halves, head_cols), F32),
            pltpu.VMEM((heads, seg, HD), BF16),
            pltpu.VMEM((STEPS, tm_count, heads, halves, 2, seg // halves, HD), BF16),
            pltpu.VMEM((seg, head_cols), BF16),
            pltpu.VMEM((heads, seg, HD), F32),
            pltpu.VMEM((heads, seg, 2 * HD), F32),
            pltpu.VMEM((s, lines, 2, rows, sw), BF16),
            pltpu.VMEM((s, lines, rows, sw), BF16),
            pltpu.VMEM((s, lines, 2, rows, sw), BF16),
            pltpu.VMEM((s, lines, 2, rows, sw), BF16),
            dma((width // gw,)),
            dma,
            dma((g, lines, 2)),
            dma((g, lines, 2)),
            dma((g, lines, 2)),
            dma((g, lines, 2)),
            dma((lines, 2)),
            dma((lines,)),
            dma((lines,)),
            dma((lines,)),
            dma((STEPS, tm_count, heads, halves)),
            dma((heads, halves)),
            dma((heads, chips, halves)),
            dma((heads, chips, halves)),
            dma((s,)),
            dma((s,)),
            dma((s, lines)),
            dma((s, lines)),
            dma((s, lines)),
            dma((s, lines)),
        ],
        compiler_params=pltpu.CompilerParams(
            collective_id=0, has_side_effects=True, vmem_limit_bytes=56 * 1024 * 1024
        ),
        cost_estimate=pl.CostEstimate(
            flops=STEPS * 2 * seg * width * head_cols * 4,
            bytes_accessed=width * head_cols * 8,
            transcendentals=STEPS * heads * seg * seg * tm_count,
        ),
    )(
        states,
        norm_gain.reshape(1, width),
        jnp.transpose(qkv_weight, (1, 0, 2)),
        qk_gain,
        out_weight,
        segment_lengths,
    )


def solution(mesh):
    return jax.shard_map(
        shards,
        mesh=mesh,
        in_specs=(
            P(("tm", "tp"), None),
            P(),
            P(None, None, "tp"),
            P(None, "tp"),
            P("tp", None),
            P(),
        ),
        out_specs=P(("tm", "tp"), None),
        check_vma=False,
    )
```

```python
import functools
import math

import jax
import jax.numpy as jnp
from jax import lax
from jax.experimental import pallas as pl
from jax.experimental.pallas import tpu as pltpu
from jax.sharding import PartitionSpec as P

HD = 128
STEPS = 2
GATHER_CHUNKS = 6
GROUP = 3
SCATTER_CHUNKS = 6
LINE_FIRST = 1

eps_norm = 1e-06
step_size = -0.5
BF16 = jnp.bfloat16
F32 = jnp.float32


def remote(src, dst, send_sem, recv_sem, tm, tp):
    return pltpu.make_async_remote_copy(
        src_ref=src,
        dst_ref=dst,
        send_sem=send_sem,
        recv_sem=recv_sem,
        device_id={"tm": tm, "tp": tp},
        device_id_type=pl.DeviceIdType.MESH,
    )


def halves_of(rows):
    return 2 if rows % 32 == 0 else 1


def loop(count, body):
    def step(index, carry):
        body(index)
        return carry

    lax.fori_loop(0, count, step, 0)


def kernel(
    tm_count, tp_count,
    states, gain, w_hbm, qk_gain, wo_hbm, lengths,
    out,
    w, wo, hb, rb, acc, qb, kv, att, run_max, run_acc, pb, yb, ub, db,
    w_sem, wo_sem,
    h_recv, h_part, h_up, h_down,
    r_recv, r_part, r_up, r_down,
    kv_recv, kv_sib, kv_chip, kv_fwd,
    y_send, y_recv, u_send, u_recv, d_send, d_recv,
):
    t, p = lax.axis_index("tm"), lax.axis_index("tp")
    lines, chips = tp_count // 2, tm_count // 2
    o, i = p // 2, p % 2
    ch, core = t // 2, t % 2
    partner, above, below = o * 2 + 1 - i, p + 2, p - 2
    sibling = ch * 2 + 1 - core
    has_above, has_below = o < lines - 1, o > 0
    rows, width = states.shape
    seg = rows * tp_count
    head_cols = w.shape[2]
    heads = head_cols // HD
    halves = halves_of(rows)
    rh, sh = rows // halves, seg // halves
    gw = width * halves // GATHER_CHUNKS
    sw = width // SCATTER_CHUNKS
    parts = width // gw
    per_gather = gw // sw
    both = GROUP

    def weight_copy(c):
        part = pl.ds(pl.multiple_of(c * gw, gw), gw)
        return pltpu.make_async_copy(w_hbm.at[:, part], w.at[:, part], w_sem.at[c])

    wo_copy = pltpu.make_async_copy(wo_hbm, wo, wo_sem)
    loop(parts, lambda c: weight_copy(c).start())
    wo_copy.start()

    barrier = pltpu.get_barrier_semaphore()

    def greet(tm, tp):
        pl.semaphore_signal(
            barrier, inc=1, device_id={"tm": tm, "tp": tp}, device_id_type=pl.DeviceIdType.MESH
        )

    greet(t, partner)
    greet(sibling, p)

    @pl.when(has_above)
    def _():
        greet(t, above)

    @pl.when(has_below)
    def _():
        greet(t, below)

    for other in range(chips):

        @pl.when(other != ch)
        def _():
            greet(other * 2 + core, p)

    out[...] = states[...]

    def prepare(c):
        part = pl.ds(pl.multiple_of(c % parts * gw, gw), gw)
        here = pl.ds(pl.multiple_of(c // parts * rh, rh), rh)
        hb[c, o, i] = (out[here, part] * gain[:, part]).astype(BF16)

    on_diagonal = lax.broadcasted_iota(
        jnp.int32, (rows, HD), 0
    ) == lax.broadcasted_iota(jnp.int32, (rows, HD), 1)

    def prepare_scale():
        square = jnp.zeros((rows, 1), F32)
        for c in range(SCATTER_CHUNKS):
            x = out[:, c * sw : (c + 1) * sw]
            square = square + jnp.sum(x * x, axis=-1, keepdims=True)
        scale = lax.rsqrt(square / width + eps_norm)
        laid = jnp.sum(jnp.where(on_diagonal, scale, 0.0), axis=0, keepdims=True)
        rb[o, i] = jnp.broadcast_to(laid, (8, HD))

    def scale_column(line, side):
        laid = jnp.broadcast_to(rb[line, side][0:1], (rows, HD))
        return jnp.sum(jnp.where(on_diagonal, laid, 0.0), axis=-1, keepdims=True)

    loop(GATHER_CHUNKS, prepare)
    prepare_scale()

    pl.semaphore_wait(
        barrier, 1 + chips + jnp.where(has_above, 1, 0) + jnp.where(has_below, 1, 0)
    )


    def h_copy(c, line, side, send_sem, tp):
        ref = hb.at[c, line, side]
        return remote(ref, ref, send_sem.at[c, line, side], h_recv.at[c, line, side], t, tp)

    def h_wait(c, line, side):
        h_copy(c, line, side, h_part, partner).wait_recv()

    def h_both_ways(c, line, side, up, down):
        if up:

            @pl.when(has_above)
            def _():
                h_copy(c, line, side, h_up, above).start()

        if down:

            @pl.when(has_below)
            def _():
                h_copy(c, line, side, h_down, below).start()

    def r_copy(line, side, send_sem, tp):
        ref = rb.at[line, side]
        return remote(ref, ref, send_sem.at[line], r_recv.at[line, side], t, tp)

    def r_forward(line, up, down):
        if up:

            @pl.when(has_above)
            def _():
                r_copy(line, i, r_up, above).start()

        if down:

            @pl.when(has_below)
            def _():
                r_copy(line, i, r_down, below).start()

        r_copy(line, i, r_part, partner).start()

    def send_own(c):
        h_both_ways(c, o, i, True, True)
        h_copy(c, o, i, h_part, partner).start()

    def kv_copy(s, seg_at, h, half, send_sem, tm):
        ref = kv.at[s, seg_at, h, half]
        return remote(ref, ref, send_sem.at[half], kv_recv.at[s, seg_at, h, half], tm, p)

    key_at = lax.broadcasted_iota(jnp.int32, (1, seg), 1)
    key_at = key_at % sh // rh * rows + key_at // sh * rh + key_at % rh
    ones = jnp.ones((seg, HD), BF16)

    def flash(s, h, segments, first):
        scores = [
            lax.dot_general(
                qb[h], kv[s, g, h, :, 0].reshape(seg, HD), (((1,), (1,)), ((), ())), preferred_element_type=F32
            )
            + jnp.where(key_at < lengths[g], 0.0, -1e30)
            for g in segments
        ]
        top = functools.reduce(jnp.maximum, scores)
        top = jnp.max(top, axis=-1, keepdims=True)
        if not first:
            old_top = run_max[h][:, :1]
            top = jnp.maximum(old_top, top)
        update = sum(
            jnp.dot(
                jnp.exp2(part - top).astype(BF16),
                jnp.concatenate([kv[s, g, h, :, 1].reshape(seg, HD), ones], axis=1),
                preferred_element_type=F32,
            )
            for part, g in zip(scores, segments)
        )
        if not first:
            update = update + run_acc[h] * jnp.exp2(old_top - top)
        run_max[h] = jnp.broadcast_to(top, (seg, HD))
        run_acc[h] = update

    def y_copy(c):
        return remote(
            pb.at[c, :, 1 - i], yb.at[c], y_send.at[c], y_recv.at[c], t, partner
        )

    def y_copy_wide(c):
        return remote(
            pb.at[c, o, 1 - i], yb.at[c, 0], y_send.at[c], y_recv.at[c], t, partner
        )

    def rows_of(buffer, c, line, wide):
        return buffer.at[c, line] if wide else buffer.at[c, line, i]

    def u_copy(c, line, wide):
        return remote(
            rows_of(pb, c, line, wide), rows_of(ub, c, line, wide),
            u_send.at[c, line], u_recv.at[c, line], t, above,
        )

    def d_copy(c, line, wide):
        return remote(
            rows_of(pb, c, line, wide), rows_of(db, c, line, wide),
            d_send.at[c, line], d_recv.at[c, line], t, below,
        )

    def step(s):
        def forward(c, distance):
            @pl.when(o >= distance)
            def _():
                line = o - distance
                h_wait(c, line, i)
                h_both_ways(c, line, i, True, False)
                h_copy(c, line, i, h_part, partner).start()

            @pl.when(o + distance < lines)
            def _():
                line = o + distance
                h_wait(c, line, i)
                h_both_ways(c, line, i, False, True)
                h_copy(c, line, i, h_part, partner).start()

        def forward_both(distance):
            for side in (i, 1 - i):

                @pl.when(o >= distance)
                def _():
                    h_wait(both, o - distance, side)
                    h_both_ways(both, o - distance, side, True, False)

                @pl.when(o + distance < lines)
                def _():
                    h_wait(both, o + distance, side)
                    h_both_ways(both, o + distance, side, False, True)

        def forward_scale(distance):
            @pl.when(o >= distance)
            def _():
                r_copy(o - distance, i, r_part, partner).wait_recv()
                r_forward(o - distance, True, False)

            @pl.when(o + distance < lines)
            def _():
                r_copy(o + distance, i, r_part, partner).wait_recv()
                r_forward(o + distance, False, True)

        def project(c):
            @pl.when(c != both)
            def _():
                for line in range(lines):
                    h_wait(c, line, 1 - i)

            @pl.when(jnp.logical_and(s == 0, c < parts))
            def _():
                weight_copy(c).wait()

            part = pl.ds(pl.multiple_of(c % parts * gw, gw), gw)
            h = hb[c].reshape(sh, gw)
            for j in range(3):
                acc[c // parts, j] += jnp.dot(h, w[j, part, :], preferred_element_type=F32)

        def scales(half):
            return jnp.concatenate(
                [
                    scale_column(line, side)[half * rh : (half + 1) * rh]
                    for line in range(lines)
                    for side in range(2)
                ],
                axis=0,
            )

        def emit_keys(half):
            scale = scales(half)
            for h in range(heads):
                cols = slice(h * HD, (h + 1) * HD)
                k = acc[half, 1, :, cols] * scale
                k_scale = lax.rsqrt(jnp.mean(k * k, axis=-1, keepdims=True) + eps_norm)
                kv[s, t, h, half, 0] = (k * k_scale * qk_gain[1:2, cols]).astype(BF16)
                kv[s, t, h, half, 1] = (acc[half, 2, :, cols] * scale).astype(BF16)
                for other in range(chips):

                    @pl.when(other > ch)
                    def _():
                        kv_copy(
                            s, t, h, half, kv_chip.at[h, other], other * 2 + core
                        ).start()

                @pl.when(core == 0)
                def _():
                    kv_copy(s, t, h, half, kv_sib.at[h], sibling).start()

        def emit_queries(half):
            scale = scales(half)
            for h in range(heads):
                cols = slice(h * HD, (h + 1) * HD)
                q = acc[half, 0, :, cols] * scale
                q_scale = lax.rsqrt(jnp.mean(q * q, axis=-1, keepdims=True) + eps_norm)
                q_scale = q_scale * (HD ** (-0.5) * math.log2(math.e))
                qb[h, half * sh : (half + 1) * sh] = (
                    q * q_scale * qk_gain[0:1, cols]
                ).astype(BF16)

        rest = GATHER_CHUNKS - GROUP - 1
        acc[...] = jnp.zeros_like(acc)
        for distance in range(1, lines - 1):
            loop(GROUP, lambda c: forward(c, distance))
            forward_scale(distance)
        loop(rest, lambda c: h_both_ways(c + both + 1, o, i, True, True))
        h_both_ways(both, o, i, True, True)
        h_wait(both, o, 1 - i)
        h_both_ways(both, o, 1 - i, True, True)
        loop(GROUP, lambda c: forward(c, lines - 1))
        forward_scale(lines - 1)
        loop(rest, lambda c: h_copy(c + both + 1, o, i, h_part, partner).start())
        for line in range(lines):
            r_copy(line, 1 - i, r_part, partner).wait_recv()

        for distance in range(1, lines - 1):

            def second(c):
                forward(c + both + 1, distance)
                if distance == 1:
                    project(c)

            loop(rest, second)
            forward_both(distance)
            if distance == 1:
                loop(GROUP - rest, lambda c: project(c + rest))
                if halves == 2:
                    emit_keys(0)
            elif distance == 2 and halves == 2:
                emit_queries(0)

        loop(rest, lambda c: forward(c + both + 1, lines - 1))

        def final(c):
            @pl.when(c == rest)
            def _():
                forward_both(lines - 1)

            project(jnp.where(c == rest, both, c + both + 1))

        loop(rest + 1, final)
        emit_keys(halves - 1)
        emit_queries(halves - 1)

        def pass_on(pair, part):
            def one(other):
                @pl.when(other < ch)
                def _():
                    for h in pair:
                        for half in part:
                            got = kv_copy(
                                s, other * 2 + core, h, half, kv_fwd.at[h, other], sibling
                            )
                            got.wait_recv()
                            got.start()

            loop(chips, one)

        pass_on(range(heads), range(halves - 1))
        for h in range(heads):
            flash(s, h, [t], True)

        @pl.when(s == 0)
        def _():
            wo_copy.wait()

        def gather_sends(c):
            def one(line):
                h_copy(c, line, i, h_part, partner).wait_send()
                way_sends(c, line, i)

            loop(lines, one)

        def scale_sends(line):
            r_copy(line, i, r_part, partner).wait_send()

            @pl.when(jnp.logical_and(has_above, line <= o))
            def _():
                r_copy(line, i, r_up, above).wait_send()

            @pl.when(jnp.logical_and(has_below, line >= o))
            def _():
                r_copy(line, i, r_down, below).wait_send()

        def way_sends(c, line, side):
            @pl.when(jnp.logical_and(has_above, line <= o))
            def _():
                h_copy(c, line, side, h_up, above).wait_send()

            @pl.when(jnp.logical_and(has_below, line >= o))
            def _():
                h_copy(c, line, side, h_down, below).wait_send()

        def both_sends(line):
            way_sends(both, line, i)
            way_sends(both, line, 1 - i)

        def chunk_sends(c):
            @pl.when(c != both)
            def _():
                gather_sends(c)

        loop(GATHER_CHUNKS, chunk_sends)
        h_copy(both, o, i, h_part, partner).wait_send()
        loop(lines, both_sends)
        loop(lines, scale_sends)

        @pl.when(core == 1)
        def _():
            for h in range(heads):
                for half in range(halves):
                    kv_copy(s, t - 1, h, half, kv_sib.at[h], sibling).wait_recv()
            for h in range(heads):
                flash(s, h, [t - 1], False)

        pairs = [range(h, min(h + 2, heads)) for h in range(0, heads, 2)]
        for pair in pairs:
            pass_on(pair, range(halves - 1, halves))

            def direct(other):
                @pl.when(other < ch)
                def _():
                    for h in pair:
                        flash(s, h, [other * 2 + core], False)

            loop(chips, direct)
        for pair in pairs:

            def passed(other):
                @pl.when(other < ch)
                def _():
                    g = other * 2 + 1 - core
                    for h in pair:
                        for half in range(halves):
                            kv_copy(s, g, h, half, kv_fwd.at[h, other], sibling).wait_recv()
                    for h in pair:
                        flash(s, h, [g], False)

            loop(chips, passed)
        for h in range(heads):
            att[:, h * HD : (h + 1) * HD] = (
                run_acc[h][:, :HD] / run_acc[h][:, HD:]
            ).astype(BF16)

        def partial(c):
            part = pl.ds(pl.multiple_of(c * sw, sw), sw)
            product = jnp.dot(att[...], wo[:, part], preferred_element_type=F32)
            for half in range(halves):
                pb[c, :, :, half * rh : (half + 1) * rh] = (
                    product[half * sh : (half + 1) * sh]
                    .astype(BF16)
                    .reshape(lines, 2, rh, sw)
                )

            @pl.when(c < LINE_FIRST)
            def _():
                start_line(c, True)

            @pl.when(c >= LINE_FIRST)
            def _():
                y_copy(c).start()

        def start_line(c, wide):
            @pl.when(o == 0)
            def _():
                for line in range(lines - 1, 0, -1):
                    u_copy(c, line, wide).start()

            @pl.when(o == lines - 1)
            def _():
                for line in range(lines - 1):
                    d_copy(c, line, wide).start()

        loop(SCATTER_CHUNKS, partial)

        def paired(c):
            y_copy(c).wait_recv()
            pb[c, :, i] = (pb[c, :, i].astype(F32) + yb[c].astype(F32)).astype(BF16)
            start_line(c, False)

        def merge(c, line, wide, buffer):
            mine, theirs = rows_of(pb, c, line, wide), rows_of(buffer, c, line, wide)
            mine[...] = (mine[...].astype(F32) + theirs[...].astype(F32)).astype(BF16)

        def hop(c, wide):
            for line in range(lines - 1, 0, -1):

                @pl.when(line > o)
                def _():
                    u_copy(c, line, wide).wait_recv()
                    merge(c, line, wide, ub)
                    u_copy(c, line, wide).start()

        def hop_down(c, wide):
            for line in range(lines - 1):

                @pl.when(line < o)
                def _():
                    d_copy(c, line, wide).wait_recv()
                    merge(c, line, wide, db)
                    d_copy(c, line, wide).start()

        def ready(k):
            @pl.when(s < STEPS - 1)
            def _():
                for half in range(halves):
                    prepare(k + half * parts)

                @pl.when(k < GROUP)
                def _():
                    send_own(k)

                @pl.when(k == both % parts)
                def _():
                    h_copy(both, o, i, h_part, partner).start()

        def finish(c, wide):
            part = pl.ds(pl.multiple_of(c * sw, sw), sw)

            @pl.when(has_below)
            def _():
                u_copy(c, o, wide).wait_recv()
                merge(c, o, wide, ub)

            @pl.when(has_above)
            def _():
                d_copy(c, o, wide).wait_recv()
                merge(c, o, wide, db)

            if wide:
                y_copy_wide(c).start()
            else:
                out[:, part] += step_size * pb[c, o, i].astype(F32)

                @pl.when(
                    jnp.logical_and(c >= per_gather, c % per_gather == per_gather - 1)
                )
                def _():
                    ready(c // per_gather)

        def tick(at):
            @pl.when(jnp.logical_and(at >= LINE_FIRST, at < SCATTER_CHUNKS))
            def _():
                paired(at)

            for k in range(1, lines):
                c = at - k
                for wide, low, high in (
                    (True, 0, LINE_FIRST),
                    (False, LINE_FIRST, SCATTER_CHUNKS),
                ):
                    live = jnp.logical_and(c >= low, c < high)
                    if k < lines - 1:

                        @pl.when(jnp.logical_and(live, o == k))
                        def _():
                            hop(c, wide)

                        @pl.when(jnp.logical_and(live, lines - 1 - o == k))
                        def _():
                            hop_down(c, wide)
                    else:

                        @pl.when(live)
                        def _():
                            finish(c, wide)

        def finish_wide(c):
            part = pl.ds(pl.multiple_of(c * sw, sw), sw)
            y_copy_wide(c).wait_recv()
            out[:, part] += step_size * (pb[c, o, i].astype(F32) + yb[c, 0].astype(F32))

        def tick_all(at):
            tick(at)

            @pl.when(at == SCATTER_CHUNKS)
            def _():
                loop(LINE_FIRST, finish_wide)
                ready(0)

        loop(SCATTER_CHUNKS + lines - 1, tick_all)

        @pl.when(s < STEPS - 1)
        def _():
            prepare_scale()
            r_forward(o, True, True)

        def scatter_sends(c):
            for wide in (True, False):

                @pl.when((c < LINE_FIRST) == wide)
                def _():
                    (y_copy_wide if wide else y_copy)(c).wait_send()

                    def one(line):
                        @pl.when(jnp.logical_and(has_above, line > o))
                        def _():
                            u_copy(c, line, wide).wait_send()

                        @pl.when(jnp.logical_and(has_below, line < o))
                        def _():
                            d_copy(c, line, wide).wait_send()

                    loop(lines, one)

        loop(SCATTER_CHUNKS, scatter_sends)
        for h in range(heads):
            for half in range(halves):

                @pl.when(core == 0)
                def _():
                    kv_copy(s, t, h, half, kv_sib.at[h], sibling).wait_send()

                def chip_sends(other):
                    @pl.when(other > ch)
                    def _():
                        kv_copy(
                            s, t, h, half, kv_chip.at[h, other], other * 2 + core
                        ).wait_send()

                    @pl.when(other < ch)
                    def _():
                        kv_copy(
                            s, other * 2 + core, h, half, kv_fwd.at[h, other], sibling
                        ).wait_send()

                loop(chips, chip_sends)

    h_copy(both, o, i, h_part, partner).start()
    for c in range(GROUP):
        send_own(c)
    r_forward(o, True, True)
    loop(STEPS, step)


def shards(states, norm_gain, qkv_weight, qk_gain, out_weight, segment_lengths):
    tm_count, tp_count = lax.axis_size("tm"), lax.axis_size("tp")
    rows, width = states.shape
    head_cols = qkv_weight.shape[2]
    heads = head_cols // HD
    seg = rows * tp_count
    lines, chips = tp_count // 2, tm_count // 2
    halves = halves_of(rows)
    gw, sw = width * halves // GATHER_CHUNKS, width // SCATTER_CHUNKS
    dma = pltpu.SemaphoreType.DMA
    vmem = pl.BlockSpec(memory_space=pltpu.VMEM)
    smem = pl.BlockSpec(memory_space=pltpu.SMEM)
    hbm = pl.BlockSpec(memory_space=pl.ANY)
    g, s = GATHER_CHUNKS, SCATTER_CHUNKS
    return pl.pallas_call(
        functools.partial(kernel, tm_count, tp_count),
        out_shape=jax.ShapeDtypeStruct((rows, width), F32),
        in_specs=[vmem, vmem, hbm, vmem, hbm, smem],
        out_specs=vmem,
        scratch_shapes=[
            pltpu.VMEM((3, width, head_cols), BF16),
            pltpu.VMEM((head_cols, width), BF16),
            pltpu.VMEM((g, lines, 2, rows // halves, gw), BF16),
            pltpu.VMEM((lines, 2, 8, HD), F32),
            pltpu.VMEM((halves, 3, seg // halves, head_cols), F32),
            pltpu.VMEM((heads, seg, HD), BF16),
            pltpu.VMEM((STEPS, tm_count, heads, halves, 2, seg // halves, HD), BF16),
            pltpu.VMEM((seg, head_cols), BF16),
            pltpu.VMEM((heads, seg, HD), F32),
            pltpu.VMEM((heads, seg, 2 * HD), F32),
            pltpu.VMEM((s, lines, 2, rows, sw), BF16),
            pltpu.VMEM((s, lines, rows, sw), BF16),
            pltpu.VMEM((s, lines, 2, rows, sw), BF16),
            pltpu.VMEM((s, lines, 2, rows, sw), BF16),
            dma((width // gw,)),
            dma,
            dma((g, lines, 2)),
            dma((g, lines, 2)),
            dma((g, lines, 2)),
            dma((g, lines, 2)),
            dma((lines, 2)),
            dma((lines,)),
            dma((lines,)),
            dma((lines,)),
            dma((STEPS, tm_count, heads, halves)),
            dma((heads, halves)),
            dma((heads, chips, halves)),
            dma((heads, chips, halves)),
            dma((s,)),
            dma((s,)),
            dma((s, lines)),
            dma((s, lines)),
            dma((s, lines)),
            dma((s, lines)),
        ],
        compiler_params=pltpu.CompilerParams(
            collective_id=0, has_side_effects=True, vmem_limit_bytes=56 * 1024 * 1024
        ),
        cost_estimate=pl.CostEstimate(
            flops=STEPS * 2 * seg * width * head_cols * 4,
            bytes_accessed=width * head_cols * 8,
            transcendentals=STEPS * heads * seg * seg * tm_count,
        ),
    )(
        states,
        norm_gain.reshape(1, width),
        jnp.transpose(qkv_weight, (1, 0, 2)),
        qk_gain,
        out_weight,
        segment_lengths,
    )


def solution(mesh):
    return jax.shard_map(
        shards,
        mesh=mesh,
        in_specs=(
            P(("tm", "tp"), None),
            P(),
            P(None, None, "tp"),
            P(None, "tp"),
            P("tp", None),
            P(),
        ),
        out_specs=P(("tm", "tp"), None),
        check_vma=False,
    )
```

```python
import functools
import math

import jax
import jax.numpy as jnp
from jax import lax
from jax.experimental import pallas as pl
from jax.experimental.pallas import tpu as pltpu
from jax.sharding import PartitionSpec as P

HD = 128
STEPS = 2
GATHER_CHUNKS = 6
GROUP = 3
SCATTER_CHUNKS = 12
LINE_FIRST = 2

eps_norm = 1e-06
step_size = -0.5
BF16 = jnp.bfloat16
F32 = jnp.float32


def remote(src, dst, send_sem, recv_sem, tm, tp):
    return pltpu.make_async_remote_copy(
        src_ref=src,
        dst_ref=dst,
        send_sem=send_sem,
        recv_sem=recv_sem,
        device_id={"tm": tm, "tp": tp},
        device_id_type=pl.DeviceIdType.MESH,
    )


def halves_of(rows):
    return 2 if rows % 32 == 0 else 1


def loop(count, body):
    def step(index, carry):
        body(index)
        return carry

    lax.fori_loop(0, count, step, 0)


def kernel(
    tm_count, tp_count,
    states, gain, w_hbm, qk_gain, wo_hbm, lengths,
    out,
    w, wo, hb, rb, acc, qb, kv, att, run_max, run_acc, pb, yb, ub, db,
    w_sem, wo_sem,
    h_recv, h_part, h_up, h_down,
    r_recv, r_part, r_up, r_down,
    kv_recv, kv_sib, kv_chip, kv_fwd,
    y_send, y_recv, u_send, u_recv, d_send, d_recv,
):
    t, p = lax.axis_index("tm"), lax.axis_index("tp")
    lines, chips = tp_count // 2, tm_count // 2
    o, i = p // 2, p % 2
    ch, core = t // 2, t % 2
    partner, above, below = o * 2 + 1 - i, p + 2, p - 2
    sibling = ch * 2 + 1 - core
    has_above, has_below = o < lines - 1, o > 0
    rows, width = states.shape
    seg = rows * tp_count
    head_cols = w.shape[2]
    heads = head_cols // HD
    halves = halves_of(rows)
    rh, sh = rows // halves, seg // halves
    gw = width * halves // GATHER_CHUNKS
    sw = width // SCATTER_CHUNKS
    parts = width // gw
    per_gather = gw // sw
    both = GROUP

    def weight_copy(c):
        part = pl.ds(pl.multiple_of(c * gw, gw), gw)
        return pltpu.make_async_copy(w_hbm.at[:, part], w.at[:, part], w_sem.at[c])

    wo_copy = pltpu.make_async_copy(wo_hbm, wo, wo_sem)
    loop(parts, lambda c: weight_copy(c).start())
    wo_copy.start()

    barrier = pltpu.get_barrier_semaphore()

    def greet(tm, tp):
        pl.semaphore_signal(
            barrier, inc=1, device_id={"tm": tm, "tp": tp}, device_id_type=pl.DeviceIdType.MESH
        )

    greet(t, partner)
    greet(sibling, p)

    @pl.when(has_above)
    def _():
        greet(t, above)

    @pl.when(has_below)
    def _():
        greet(t, below)

    for other in range(chips):

        @pl.when(other != ch)
        def _():
            greet(other * 2 + core, p)

    out[...] = states[...]

    def prepare(c):
        part = pl.ds(pl.multiple_of(c % parts * gw, gw), gw)
        here = pl.ds(pl.multiple_of(c // parts * rh, rh), rh)
        hb[c, o, i] = (out[here, part] * gain[:, part]).astype(BF16)

    on_diagonal = lax.broadcasted_iota(
        jnp.int32, (rows, HD), 0
    ) == lax.broadcasted_iota(jnp.int32, (rows, HD), 1)

    def prepare_scale():
        square = jnp.zeros((rows, 1), F32)
        for c in range(SCATTER_CHUNKS):
            x = out[:, c * sw : (c + 1) * sw]
            square = square + jnp.sum(x * x, axis=-1, keepdims=True)
        scale = lax.rsqrt(square / width + eps_norm)
        laid = jnp.sum(jnp.where(on_diagonal, scale, 0.0), axis=0, keepdims=True)
        rb[o, i] = jnp.broadcast_to(laid, (8, HD))

    def scale_column(line, side):
        laid = jnp.broadcast_to(rb[line, side][0:1], (rows, HD))
        return jnp.sum(jnp.where(on_diagonal, laid, 0.0), axis=-1, keepdims=True)

    loop(GATHER_CHUNKS, prepare)
    prepare_scale()

    pl.semaphore_wait(
        barrier, 1 + chips + jnp.where(has_above, 1, 0) + jnp.where(has_below, 1, 0)
    )


    def h_copy(c, line, side, send_sem, tp):
        ref = hb.at[c, line, side]
        return remote(ref, ref, send_sem.at[c, line, side], h_recv.at[c, line, side], t, tp)

    def h_wait(c, line, side):
        h_copy(c, line, side, h_part, partner).wait_recv()

    def h_both_ways(c, line, side, up, down):
        if up:

            @pl.when(has_above)
            def _():
                h_copy(c, line, side, h_up, above).start()

        if down:

            @pl.when(has_below)
            def _():
                h_copy(c, line, side, h_down, below).start()

    def r_copy(line, side, send_sem, tp):
        ref = rb.at[line, side]
        return remote(ref, ref, send_sem.at[line], r_recv.at[line, side], t, tp)

    def r_forward(line, up, down):
        if up:

            @pl.when(has_above)
            def _():
                r_copy(line, i, r_up, above).start()

        if down:

            @pl.when(has_below)
            def _():
                r_copy(line, i, r_down, below).start()

        r_copy(line, i, r_part, partner).start()

    def send_own(c):
        h_both_ways(c, o, i, True, True)
        h_copy(c, o, i, h_part, partner).start()

    def kv_copy(s, seg_at, h, half, send_sem, tm):
        ref = kv.at[s, seg_at, h, half]
        return remote(ref, ref, send_sem.at[half], kv_recv.at[s, seg_at, h, half], tm, p)

    key_at = lax.broadcasted_iota(jnp.int32, (1, seg), 1)
    key_at = key_at % sh // rh * rows + key_at // sh * rh + key_at % rh
    ones = jnp.ones((seg, HD), BF16)

    def flash(s, h, segments, first):
        scores = [
            lax.dot_general(
                qb[h], kv[s, g, h, :, 0].reshape(seg, HD), (((1,), (1,)), ((), ())), preferred_element_type=F32
            )
            + jnp.where(key_at < lengths[g], 0.0, -1e30)
            for g in segments
        ]
        top = functools.reduce(jnp.maximum, scores)
        top = jnp.max(top, axis=-1, keepdims=True)
        if not first:
            old_top = run_max[h][:, :1]
            top = jnp.maximum(old_top, top)
        update = sum(
            jnp.dot(
                jnp.exp2(part - top).astype(BF16),
                jnp.concatenate([kv[s, g, h, :, 1].reshape(seg, HD), ones], axis=1),
                preferred_element_type=F32,
            )
            for part, g in zip(scores, segments)
        )
        if not first:
            update = update + run_acc[h] * jnp.exp2(old_top - top)
        run_max[h] = jnp.broadcast_to(top, (seg, HD))
        run_acc[h] = update

    def y_copy(c):
        return remote(
            pb.at[c, :, 1 - i], yb.at[c], y_send.at[c], y_recv.at[c], t, partner
        )

    def y_copy_wide(c):
        return remote(
            pb.at[c, o, 1 - i], yb.at[c, 0], y_send.at[c], y_recv.at[c], t, partner
        )

    def rows_of(buffer, c, line, wide):
        return buffer.at[c, line] if wide else buffer.at[c, line, i]

    def u_copy(c, k, wide):
        lines_on = pl.ds(k + 1, lines - 1 - k)
        return remote(
            rows_of(pb, c, lines_on, wide), rows_of(ub, c, lines_on, wide),
            u_send.at[c, 0], u_recv.at[c, 0], t, above,
        )

    def d_copy(c, k, wide):
        lines_on = pl.ds(0, k)
        return remote(
            rows_of(pb, c, lines_on, wide), rows_of(db, c, lines_on, wide),
            d_send.at[c, 0], d_recv.at[c, 0], t, below,
        )

    def step(s):
        def forward(c, distance):
            @pl.when(o >= distance)
            def _():
                line = o - distance
                h_wait(c, line, i)
                h_both_ways(c, line, i, True, False)
                h_copy(c, line, i, h_part, partner).start()

            @pl.when(o + distance < lines)
            def _():
                line = o + distance
                h_wait(c, line, i)
                h_both_ways(c, line, i, False, True)
                h_copy(c, line, i, h_part, partner).start()

        def forward_both(distance):
            for side in (i, 1 - i):

                @pl.when(o >= distance)
                def _():
                    h_wait(both, o - distance, side)
                    h_both_ways(both, o - distance, side, True, False)

                @pl.when(o + distance < lines)
                def _():
                    h_wait(both, o + distance, side)
                    h_both_ways(both, o + distance, side, False, True)

        def forward_scale(distance):
            @pl.when(o >= distance)
            def _():
                r_copy(o - distance, i, r_part, partner).wait_recv()
                r_forward(o - distance, True, False)

            @pl.when(o + distance < lines)
            def _():
                r_copy(o + distance, i, r_part, partner).wait_recv()
                r_forward(o + distance, False, True)

        def project(c):
            @pl.when(c != both)
            def _():
                for line in range(lines):
                    h_wait(c, line, 1 - i)

            @pl.when(jnp.logical_and(s == 0, c < parts))
            def _():
                weight_copy(c).wait()

            part = pl.ds(pl.multiple_of(c % parts * gw, gw), gw)
            h = hb[c].reshape(sh, gw)
            for j in range(3):
                acc[c // parts, j] += jnp.dot(h, w[j, part, :], preferred_element_type=F32)

        def scales(half):
            return jnp.concatenate(
                [
                    scale_column(line, side)[half * rh : (half + 1) * rh]
                    for line in range(lines)
                    for side in range(2)
                ],
                axis=0,
            )

        def emit_keys(half):
            scale = scales(half)
            for h in range(heads):
                cols = slice(h * HD, (h + 1) * HD)
                k = acc[half, 1, :, cols] * scale
                k_scale = lax.rsqrt(jnp.mean(k * k, axis=-1, keepdims=True) + eps_norm)
                kv[s, t, h, half, 0] = (k * k_scale * qk_gain[1:2, cols]).astype(BF16)
                kv[s, t, h, half, 1] = (acc[half, 2, :, cols] * scale).astype(BF16)
                for other in range(chips):

                    @pl.when(other > ch)
                    def _():
                        kv_copy(
                            s, t, h, half, kv_chip.at[h, other], other * 2 + core
                        ).start()

                @pl.when(core == 0)
                def _():
                    kv_copy(s, t, h, half, kv_sib.at[h], sibling).start()

        def emit_queries(half):
            scale = scales(half)
            for h in range(heads):
                cols = slice(h * HD, (h + 1) * HD)
                q = acc[half, 0, :, cols] * scale
                q_scale = lax.rsqrt(jnp.mean(q * q, axis=-1, keepdims=True) + eps_norm)
                q_scale = q_scale * (HD ** (-0.5) * math.log2(math.e))
                qb[h, half * sh : (half + 1) * sh] = (
                    q * q_scale * qk_gain[0:1, cols]
                ).astype(BF16)

        rest = GATHER_CHUNKS - GROUP - 1
        acc[...] = jnp.zeros_like(acc)
        for distance in range(1, lines - 1):
            loop(GROUP, lambda c: forward(c, distance))
            forward_scale(distance)
        loop(rest, lambda c: h_both_ways(c + both + 1, o, i, True, True))
        h_both_ways(both, o, i, True, True)
        h_wait(both, o, 1 - i)
        h_both_ways(both, o, 1 - i, True, True)
        loop(GROUP, lambda c: forward(c, lines - 1))
        forward_scale(lines - 1)
        loop(rest, lambda c: h_copy(c + both + 1, o, i, h_part, partner).start())
        for line in range(lines):
            r_copy(line, 1 - i, r_part, partner).wait_recv()

        for distance in range(1, lines - 1):

            def second(c):
                forward(c + both + 1, distance)
                if distance == 1:
                    project(c)

            loop(rest, second)
            forward_both(distance)
            if distance == 1:
                loop(GROUP - rest, lambda c: project(c + rest))
                if halves == 2:
                    emit_keys(0)
            elif distance == 2 and halves == 2:
                emit_queries(0)

        loop(rest, lambda c: forward(c + both + 1, lines - 1))

        def final(c):
            @pl.when(c == rest)
            def _():
                forward_both(lines - 1)

            project(jnp.where(c == rest, both, c + both + 1))

        loop(rest + 1, final)
        emit_keys(halves - 1)
        emit_queries(halves - 1)

        def pass_on(pair, part):
            def one(other):
                @pl.when(other < ch)
                def _():
                    for h in pair:
                        for half in part:
                            got = kv_copy(
                                s, other * 2 + core, h, half, kv_fwd.at[h, other], sibling
                            )
                            got.wait_recv()
                            got.start()

            loop(chips, one)

        pass_on(range(heads), range(halves - 1))
        for h in range(heads):
            flash(s, h, [t], True)

        @pl.when(s == 0)
        def _():
            wo_copy.wait()

        def gather_sends(c):
            def one(line):
                h_copy(c, line, i, h_part, partner).wait_send()
                way_sends(c, line, i)

            loop(lines, one)

        def scale_sends(line):
            r_copy(line, i, r_part, partner).wait_send()

            @pl.when(jnp.logical_and(has_above, line <= o))
            def _():
                r_copy(line, i, r_up, above).wait_send()

            @pl.when(jnp.logical_and(has_below, line >= o))
            def _():
                r_copy(line, i, r_down, below).wait_send()

        def way_sends(c, line, side):
            @pl.when(jnp.logical_and(has_above, line <= o))
            def _():
                h_copy(c, line, side, h_up, above).wait_send()

            @pl.when(jnp.logical_and(has_below, line >= o))
            def _():
                h_copy(c, line, side, h_down, below).wait_send()

        def both_sends(line):
            way_sends(both, line, i)
            way_sends(both, line, 1 - i)

        def chunk_sends(c):
            @pl.when(c != both)
            def _():
                gather_sends(c)

        loop(GATHER_CHUNKS, chunk_sends)
        h_copy(both, o, i, h_part, partner).wait_send()
        loop(lines, both_sends)
        loop(lines, scale_sends)

        @pl.when(core == 1)
        def _():
            for h in range(heads):
                for half in range(halves):
                    kv_copy(s, t - 1, h, half, kv_sib.at[h], sibling).wait_recv()
            for h in range(heads):
                flash(s, h, [t - 1], False)

        pairs = [range(h, min(h + 2, heads)) for h in range(0, heads, 2)]
        for pair in pairs:
            pass_on(pair, range(halves - 1, halves))

            def direct(other):
                @pl.when(other < ch)
                def _():
                    for h in pair:
                        flash(s, h, [other * 2 + core], False)

            loop(chips, direct)
        for pair in pairs:

            def passed(other):
                @pl.when(other < ch)
                def _():
                    g = other * 2 + 1 - core
                    for h in pair:
                        for half in range(halves):
                            kv_copy(s, g, h, half, kv_fwd.at[h, other], sibling).wait_recv()
                    for h in pair:
                        flash(s, h, [g], False)

            loop(chips, passed)
        for h in range(heads):
            att[:, h * HD : (h + 1) * HD] = (
                run_acc[h][:, :HD] / run_acc[h][:, HD:]
            ).astype(BF16)

        def partial(c):
            part = pl.ds(pl.multiple_of(c * sw, sw), sw)
            product = jnp.dot(att[...], wo[:, part], preferred_element_type=F32)
            for half in range(halves):
                pb[c, :, :, half * rh : (half + 1) * rh] = (
                    product[half * sh : (half + 1) * sh]
                    .astype(BF16)
                    .reshape(lines, 2, rh, sw)
                )

            @pl.when(c < LINE_FIRST)
            def _():
                start_line(c, True)

            @pl.when(c >= LINE_FIRST)
            def _():
                y_copy(c).start()

        def start_line(c, wide):
            @pl.when(o == 0)
            def _():
                u_copy(c, 0, wide).start()

            @pl.when(o == lines - 1)
            def _():
                d_copy(c, lines - 1, wide).start()

        loop(SCATTER_CHUNKS, partial)

        def paired(c):
            y_copy(c).wait_recv()
            pb[c, :, i] = (pb[c, :, i].astype(F32) + yb[c].astype(F32)).astype(BF16)
            start_line(c, False)

        def merge(c, line, wide, buffer):
            mine, theirs = rows_of(pb, c, line, wide), rows_of(buffer, c, line, wide)
            mine[...] = (mine[...].astype(F32) + theirs[...].astype(F32)).astype(BF16)

        def hop(c, k, wide):
            u_copy(c, k - 1, wide).wait_recv()
            for line in range(k + 1, lines):
                merge(c, line, wide, ub)
            u_copy(c, k, wide).start()

        def hop_down(c, k, wide):
            d_copy(c, k + 1, wide).wait_recv()
            for line in range(k):
                merge(c, line, wide, db)
            d_copy(c, k, wide).start()

        def ready(k):
            @pl.when(s < STEPS - 1)
            def _():
                for half in range(halves):
                    prepare(k + half * parts)

                @pl.when(k < GROUP)
                def _():
                    send_own(k)

                @pl.when(k == both % parts)
                def _():
                    h_copy(both, o, i, h_part, partner).start()

        def finish(c, wide):
            part = pl.ds(pl.multiple_of(c * sw, sw), sw)

            @pl.when(o == lines - 1)
            def _():
                u_copy(c, lines - 2, wide).wait_recv()

            @pl.when(o == 0)
            def _():
                d_copy(c, 1, wide).wait_recv()

            @pl.when(has_below)
            def _():
                merge(c, o, wide, ub)

            @pl.when(has_above)
            def _():
                merge(c, o, wide, db)

            if wide:
                y_copy_wide(c).start()
            else:
                out[:, part] += step_size * pb[c, o, i].astype(F32)

                @pl.when(
                    jnp.logical_and(c >= per_gather, c % per_gather == per_gather - 1)
                )
                def _():
                    ready(c // per_gather)

        def tick(at):
            @pl.when(jnp.logical_and(at >= LINE_FIRST, at < SCATTER_CHUNKS))
            def _():
                paired(at)

            for k in range(1, lines):
                c = at - k
                for wide, low, high in (
                    (True, 0, LINE_FIRST),
                    (False, LINE_FIRST, SCATTER_CHUNKS),
                ):
                    live = jnp.logical_and(c >= low, c < high)
                    if k < lines - 1:

                        @pl.when(jnp.logical_and(live, o == k))
                        def _():
                            hop(c, k, wide)

                        @pl.when(jnp.logical_and(live, lines - 1 - o == k))
                        def _():
                            hop_down(c, lines - 1 - k, wide)
                    else:

                        @pl.when(live)
                        def _():
                            finish(c, wide)

        def finish_wide(c):
            part = pl.ds(pl.multiple_of(c * sw, sw), sw)
            y_copy_wide(c).wait_recv()
            out[:, part] += step_size * (pb[c, o, i].astype(F32) + yb[c, 0].astype(F32))

        def tick_all(at):
            tick(at)

            @pl.when(at == SCATTER_CHUNKS)
            def _():
                loop(LINE_FIRST, finish_wide)
                ready(0)

        loop(SCATTER_CHUNKS + lines - 1, tick_all)

        @pl.when(s < STEPS - 1)
        def _():
            prepare_scale()
            r_forward(o, True, True)

        def scatter_sends(c):
            for wide in (True, False):

                @pl.when((c < LINE_FIRST) == wide)
                def _():
                    (y_copy_wide if wide else y_copy)(c).wait_send()

                    for k in range(lines):

                        @pl.when(o == k)
                        def _():
                            if k < lines - 1:
                                u_copy(c, k, wide).wait_send()
                            if k > 0:
                                d_copy(c, k, wide).wait_send()

        loop(SCATTER_CHUNKS, scatter_sends)
        for h in range(heads):
            for half in range(halves):

                @pl.when(core == 0)
                def _():
                    kv_copy(s, t, h, half, kv_sib.at[h], sibling).wait_send()

                def chip_sends(other):
                    @pl.when(other > ch)
                    def _():
                        kv_copy(
                            s, t, h, half, kv_chip.at[h, other], other * 2 + core
                        ).wait_send()

                    @pl.when(other < ch)
                    def _():
                        kv_copy(
                            s, other * 2 + core, h, half, kv_fwd.at[h, other], sibling
                        ).wait_send()

                loop(chips, chip_sends)

    h_copy(both, o, i, h_part, partner).start()
    for c in range(GROUP):
        send_own(c)
    r_forward(o, True, True)
    loop(STEPS, step)


def shards(states, norm_gain, qkv_weight, qk_gain, out_weight, segment_lengths):
    tm_count, tp_count = lax.axis_size("tm"), lax.axis_size("tp")
    rows, width = states.shape
    head_cols = qkv_weight.shape[2]
    heads = head_cols // HD
    seg = rows * tp_count
    lines, chips = tp_count // 2, tm_count // 2
    halves = halves_of(rows)
    gw, sw = width * halves // GATHER_CHUNKS, width // SCATTER_CHUNKS
    dma = pltpu.SemaphoreType.DMA
    vmem = pl.BlockSpec(memory_space=pltpu.VMEM)
    smem = pl.BlockSpec(memory_space=pltpu.SMEM)
    hbm = pl.BlockSpec(memory_space=pl.ANY)
    g, s = GATHER_CHUNKS, SCATTER_CHUNKS
    return pl.pallas_call(
        functools.partial(kernel, tm_count, tp_count),
        out_shape=jax.ShapeDtypeStruct((rows, width), F32),
        in_specs=[vmem, vmem, hbm, vmem, hbm, smem],
        out_specs=vmem,
        scratch_shapes=[
            pltpu.VMEM((3, width, head_cols), BF16),
            pltpu.VMEM((head_cols, width), BF16),
            pltpu.VMEM((g, lines, 2, rows // halves, gw), BF16),
            pltpu.VMEM((lines, 2, 8, HD), F32),
            pltpu.VMEM((halves, 3, seg // halves, head_cols), F32),
            pltpu.VMEM((heads, seg, HD), BF16),
            pltpu.VMEM((STEPS, tm_count, heads, halves, 2, seg // halves, HD), BF16),
            pltpu.VMEM((seg, head_cols), BF16),
            pltpu.VMEM((heads, seg, HD), F32),
            pltpu.VMEM((heads, seg, 2 * HD), F32),
            pltpu.VMEM((s, lines, 2, rows, sw), BF16),
            pltpu.VMEM((s, lines, rows, sw), BF16),
            pltpu.VMEM((s, lines, 2, rows, sw), BF16),
            pltpu.VMEM((s, lines, 2, rows, sw), BF16),
            dma((width // gw,)),
            dma,
            dma((g, lines, 2)),
            dma((g, lines, 2)),
            dma((g, lines, 2)),
            dma((g, lines, 2)),
            dma((lines, 2)),
            dma((lines,)),
            dma((lines,)),
            dma((lines,)),
            dma((STEPS, tm_count, heads, halves)),
            dma((heads, halves)),
            dma((heads, chips, halves)),
            dma((heads, chips, halves)),
            dma((s,)),
            dma((s,)),
            dma((s, lines)),
            dma((s, lines)),
            dma((s, lines)),
            dma((s, lines)),
        ],
        compiler_params=pltpu.CompilerParams(
            collective_id=0, has_side_effects=True, vmem_limit_bytes=56 * 1024 * 1024
        ),
        cost_estimate=pl.CostEstimate(
            flops=STEPS * 2 * seg * width * head_cols * 4,
            bytes_accessed=width * head_cols * 8,
            transcendentals=STEPS * heads * seg * seg * tm_count,
        ),
    )(
        states,
        norm_gain.reshape(1, width),
        jnp.transpose(qkv_weight, (1, 0, 2)),
        qk_gain,
        out_weight,
        segment_lengths,
    )


def solution(mesh):
    return jax.shard_map(
        shards,
        mesh=mesh,
        in_specs=(
            P(("tm", "tp"), None),
            P(),
            P(None, None, "tp"),
            P(None, "tp"),
            P("tp", None),
            P(),
        ),
        out_specs=P(("tm", "tp"), None),
        check_vma=False,
    )
```
